128 devices in a mesh: gz: 8 (over y, x_hi), gy: 16 (over z, x_lo, core).
Axes of the slice: x: 4 (x_hi: 2, x_lo: 2; x = x_hi * 2 + x_lo), y: 4, z: 4, core: 2. Of those that a mesh axis runs over, the one named last changes fastest.
Arguments:
- velocity: float32 [128, 1024, 1024], P(None, 'gy', 'gz'), may hold values from -6 to 6
Outputs:
- fine_details: float32 [7, 64, 512, 512], P(None, None, 'gy', 'gz')
- coarse_bands: float32 [8, 32, 256, 256], P(None, None, 'gy', 'gz')
The draws below stay inside these ranges and needn't reach their ends.
All inputs are finite; a program needn't handle non-finite values.
Results may differ from the reference program's by a relative error of at most 0.0003.
Values sent between devices are 32-bit elements; how exact they have to be, the bound alone decides.
A program may use at most 192 MiB of HBM per device.

```python
from functools import partial
import jax
import jax.numpy as jnp
from jax import lax

CX = 128
NY = 1024
NZ = 1024


def levels(key, extent, split, least, top_value):
    loudness = 1.0
    for position, blocks in split:
        draws = jax.random.uniform(jax.random.fold_in(jax.random.fold_in(key, 6), position), (blocks,), jnp.float32, least / len(split), top_value / len(split))
        loudness = loudness * jnp.repeat(jnp.exp(draws), extent[position] // blocks).reshape((-1,) + (1,) * (len(extent) - 1 - position))
    return loudness


def centred(own_key, extent, width, reach, cuts=(), dtype=jnp.bfloat16):
    drawn = jax.random.normal(own_key, extent, jnp.float32) * width
    if len(cuts) > 0:
        drawn = levels(own_key, extent, cuts, -0.22, 0.18) * drawn
    return jnp.clip(drawn, min=-reach, max=reach).astype(dtype)


def setup_inputs(seed: int = 0) -> dict:
    keys = jax.random.split(jax.random.key(seed), 2)
    return {
        "velocity": centred(keys[0], (CX, NY, NZ), 1.0, 6.0, ((1, 16), (2, 8)), jnp.float32),
    }


predict_one = -1.586134342
update_one = -0.05298011854
predict_two = 0.8829110762
update_two = 0.4435068522
scale_factor = 1.149604398


def lift_axis(field, axis_index, take_next, take_prev):
    length = field.shape[axis_index]
    new_shape = field.shape[:axis_index] + (length // 2, 2) + field.shape[axis_index + 1:]
    paired = field.reshape(new_shape)
    even_part = lax.index_in_dim(paired, 0, axis_index + 1, keepdims=False)
    odd_part = lax.index_in_dim(paired, 1, axis_index + 1, keepdims=False)
    odd_part = odd_part + predict_one * (even_part + take_next(even_part))
    even_part = even_part + update_one * (take_prev(odd_part) + odd_part)
    odd_part = odd_part + predict_two * (even_part + take_next(even_part))
    even_part = even_part + update_two * (take_prev(odd_part) + odd_part)
    return jnp.stack([even_part * scale_factor, odd_part / scale_factor], axis=axis_index)


def rolled_next(values_in, axis_index):
    return jnp.roll(values_in, -1, axis=axis_index)


def rolled_prev(values_in, axis_index):
    return jnp.roll(values_in, 1, axis=axis_index)


def lift_periodic(field, axis_index):
    return lift_axis(field, axis_index, partial(rolled_next, axis_index=axis_index), partial(rolled_prev, axis_index=axis_index))


def transform_level(volume):
    along_x = lift_periodic(volume, 0)
    along_y = lift_periodic(along_x, 2)
    along_z = lift_periodic(along_y, 4)
    bands = jnp.transpose(along_z, (0, 2, 4, 1, 3, 5))
    return bands.reshape((8,) + bands.shape[3:])


def reference(velocity):
    level_one = transform_level(velocity)
    level_two = transform_level(level_one[0])
    return level_one[1:], level_two
```

```python
import functools

import jax
import jax.numpy as jnp
import ml_dtypes
import numpy as np
from jax import lax
from jax.experimental import pallas as pl
from jax.experimental.pallas import tpu as pltpu
from jax.sharding import PartitionSpec as P

predict_one = -1.586134342
update_one = -0.05298011854
predict_two = 0.8829110762
update_two = 0.4435068522
scale_factor = 1.149604398

MESH = pl.DeviceIdType.MESH
F32 = jnp.float32
BF16 = jnp.bfloat16
NX, HX = 128, 64
BY, BZ = 64, 128
LOW_ROWS, HIGH_ROWS = 4 * HX, 2 * HX


def lift_rows(v):
    s, d = v[0::2], v[1::2]
    d = d + predict_one * (s + np.roll(s, -1, 0))
    s = s + update_one * (np.roll(d, 1, 0) + d)
    d = d + predict_two * (s + np.roll(s, -1, 0))
    s = s + update_two * (np.roll(d, 1, 0) + d)
    return s * scale_factor, d / scale_factor


def factored(block, fine):
    first = np.linalg.svd(block[:fine])[2][:2]
    rest = block[fine:] - (block[fine:] @ first.T) @ first
    second = np.linalg.svd(rest)[2][:2]
    basis = np.concatenate([first, second])
    gains = block @ basis.T
    gains[:fine, 2:] = 0
    return basis, gains


@functools.cache
def operators(n):
    low, high = lift_rows(np.eye(3 * n))
    low2, high2 = lift_rows(low)
    h, q = n // 2, n // 4
    rows = np.concatenate([low[h : 2 * h], high[h : 2 * h], low2[q : 2 * q], high2[q : 2 * q]])
    return rows[:, n : 2 * n], factored(rows[:, :n], n), factored(rows[:, 2 * n :], n)


def halves(w):
    hi = w.astype(ml_dtypes.bfloat16)
    return hi, (w - hi.astype(np.float64)).astype(ml_dtypes.bfloat16)


def three(w, axis):
    hi, lo = halves(w)
    return np.concatenate([hi, hi, lo], axis)


@functools.cache
def constants():
    own_y, (basis_left, gain_left), (basis_right, gain_right) = operators(BY)
    y_low = np.zeros((2, 96, 80))
    y_high = np.zeros((4, 64, 80))
    for p in range(2):
        y_low[p, :, :64] = own_y
        y_low[p, :, 64 + 4 * p : 68 + 4 * p] = gain_left
        y_low[p, :, 72 + 4 * p : 76 + 4 * p] = gain_right
    for p in range(4):
        y_high[p, :, :64] = own_y[:64]
        y_high[p, :, 64 + 2 * p : 66 + 2 * p] = gain_left[:64, :2]
        y_high[p, :, 72 + 2 * p : 74 + 2 * p] = gain_right[:64, :2]
    edge = np.r_[0:16, 48:64]
    assert abs(np.delete(basis_left, edge, 1)).max() < 1e-12
    assert abs(np.delete(basis_right, edge, 1)).max() < 1e-12
    state_low = np.zeros((64, 256))
    state_high = np.zeros((32, 256))
    for side, basis in enumerate((basis_right, basis_left)):
        for i in range(8):
            columns = slice(32 * i, 32 * i + 32)
            state_low[32 * side + 4 * i : 32 * side + 4 * i + 4, columns] = basis[:, edge]
            state_high[16 * side + 2 * i : 16 * side + 2 * i + 2, columns] = basis[:2, edge]

    own_z, (left, gain_l), (right, gain_r) = operators(BZ)
    zs_low = np.concatenate([np.tile(b.T, (1, 32)) for b in (right, left)], 1)
    zs_high = np.concatenate([np.tile(b[:2].T, (1, 64)) for b in (right, left)], 1)

    def spread(rows):
        k = rows.shape[1]
        fine = np.zeros((k, 256))
        fine[:, :64] = rows[:64].T
        fine[:, 128:192] = rows[64:128].T
        coarse = np.zeros((k, 128))
        coarse[:, :64] = rows[128:].T
        return fine, coarse

    main_fine, main_coarse = spread(own_z)
    halo_fine, halo_coarse = spread(np.concatenate([gain_l, gain_r], 1))

    def passes(main, halo):
        hi, lo = halves(main)
        ehi, elo = halves(halo)
        one = np.concatenate([hi, hi], 0)
        two = np.zeros((4, 256, main.shape[1]), ml_dtypes.bfloat16)
        for i in range(4):
            two[i, :128] = lo
            two[i, 128 + 32 * i : 128 + 32 * i + 24] = np.concatenate([ehi, ehi, elo], 0)
        return one, two

    def places(states):
        p = np.zeros((4, 128, 128))
        for lane in range(128):
            i, s = lane // states % 4, lane % states
            p[0, lane, 32 * i + s] = p[0, lane, 32 * i + 16 + s] = 1
            p[1, lane, 32 * i + 8 + s] = 1
            p[2, lane, 32 * i + 4 + s] = p[2, lane, 32 * i + 20 + s] = 1
            p[3, lane, 32 * i + 12 + s] = 1
        return p.reshape(512, 128).astype(ml_dtypes.bfloat16)

    w1, w2 = passes(main_fine, halo_fine)
    w1c, w2c = passes(main_coarse, halo_coarse)
    send = (three(state_low, 1), three(state_high, 1), three(zs_low, 0), three(zs_high, 0))
    work = (three(y_low, 2), three(y_high, 2), w1, w2, w1c, w2c, places(4), places(2))
    return send, work


def split(v):
    hi = v.astype(BF16)
    return hi, (v - hi.astype(F32)).astype(BF16)


def dot(a, b):
    return jnp.dot(a, b, preferred_element_type=F32)


def lift_loop(count, unroll, load, store):
    k = 2 * count
    s_a, d_a, s_b, d_b, s_c, d_c, s_d = [load(i % k) for i in range(k - 4, k + 3)]
    d_a = d_a + predict_one * (s_a + s_b)
    d_b = d_b + predict_one * (s_b + s_c)
    s_b = s_b + update_one * (d_a + d_b)
    d_c = d_c + predict_one * (s_c + s_d)
    s_c = s_c + update_one * (d_b + d_c)
    d_b = d_b + predict_two * (s_b + s_c)

    def step(j, carry):
        s_now, d_before, s_before, d_done = carry
        for u in range(unroll):
            n = unroll * j + u + 1
            d_now, s_next = load(lax.rem(2 * n + 1, k)), load(lax.rem(2 * n + 2, k))
            d_now = d_now + predict_one * (s_now + s_next)
            s_now = s_now + update_one * (d_before + d_now)
            d_before = d_before + predict_two * (s_before + s_now)
            s_before = s_before + update_two * (d_done + d_before)
            store(n - 1, s_before * scale_factor, d_before * (1.0 / scale_factor))
            s_now, d_before, s_before, d_done = s_next, d_now, s_now, d_before
        return s_now, d_before, s_before, d_done

    lax.fori_loop(0, count // unroll, step, (s_d, d_c, s_c, d_b))


def exchange_kernel(
    v_hbm, st_low, st_high, zs_low, zs_high,
    x_hi, x_lo, y_recv, z_recv, c_recv,
    v, y_send, z_send, c_send, in_sem, send_sem, recv_sem,
):
    my_y, my_z = lax.axis_index("gy"), lax.axis_index("gz")
    n_y, n_z = lax.axis_size("gy"), lax.axis_size("gz")

    def device(step_y, step_z):
        return {
            "gy": lax.rem(my_y + step_y + n_y, n_y),
            "gz": lax.rem(my_z + step_z + n_z, n_z),
        }

    steps = [(0, -1), (0, 1), (-1, 0), (1, 0), (-1, -1), (-1, 1), (1, -1), (1, 1)]
    barrier = pltpu.get_barrier_semaphore()
    for step in steps:
        pl.semaphore_signal(barrier, inc=1, device_id=device(*step), device_id_type=MESH)

    order = (0, 3, 1, 2)
    loads = {}
    for c in order:
        rows = pl.ds(16 * c, 16)
        loads[c] = pltpu.make_async_copy(v_hbm.at[:, rows], v.at[:, rows], in_sem.at[c])
        loads[c].start()

    for c in order:
        loads[c].wait()
        rows = pl.ds(16 * c, 16)

        def store(n, low, high, rows=rows):
            x_hi[n, rows], x_lo[n, rows] = split(low)
            x_hi[HX + n, rows], x_lo[HX + n, rows] = split(high)

        lift_loop(HX, 4, lambda i, rows=rows: v[i, rows], store)

    def y_states(g, carry):
        for half, table, per in ((0, st_low, 4), (1, st_high, 2)):
            first = HX * half + 8 * g
            parts = []
            for ref in (x_hi, x_lo):
                for i in range(8):
                    parts += [ref[first + i, 0:16], ref[first + i, 48:64]]
            parts += parts[:16]
            states = dot(table[...], jnp.concatenate(parts, 0))
            n = 8 * per
            at = pl.ds(pl.multiple_of(LOW_ROWS * half + n * g, n), n)
            y_send[0, at] = states[:n]
            y_send[1, at] = states[n:]
        return carry

    lax.fori_loop(0, 8, y_states, 0)

    lane = lax.broadcasted_iota(jnp.int32, (64, 256), 1) % 128
    for group, (first, count, table, per) in enumerate(
        ((0, 32, zs_low, 4), (32, 32, zs_low, 4), (64, 64, zs_high, 2))
    ):

        def z_states(j, acc, first=first, table=table, per=per):
            hi = x_hi[pl.ds(first + 8 * j, 8)].reshape(512, 128)
            lo = x_lo[pl.ds(first + 8 * j, 8)].reshape(512, 128)
            states = dot(jnp.concatenate([hi, lo, hi], 1), table[...])
            for i in range(8):
                mine = lane // per == 8 * j + i
                acc = jnp.where(mine, states[64 * i : 64 * i + 64], acc)
            return acc

        acc = lax.fori_loop(0, count // 8, z_states, jnp.zeros((64, 256), F32))
        z_send[0, 64 * group : 64 * group + 64] = acc[:, :128]
        z_send[1, 64 * group : 64 * group + 64] = acc[:, 128:]

    his, los = [], []
    zeros = jnp.zeros((32, 128), F32)
    for side in range(2):
        for group in range(4):
            if group == 3:
                piece = zeros
            else:
                at = 64 * group
                piece = jnp.concatenate(
                    [z_send[side, at : at + 16], z_send[side, at + 48 : at + 64]], 0
                )
            hi, lo = split(piece)
            his.append(hi)
            los.append(lo)
    c_send[...] = dot(st_low[...], jnp.concatenate(his + los + his, 0)).reshape(4, 16, 128)

    pl.semaphore_wait(barrier, 8)
    copies = []
    for k, step in enumerate(steps):
        if k < 2:
            source, target = z_send.at[k], z_recv.at[1 - k]
        elif k < 4:
            source, target = y_send.at[k - 2], y_recv.at[3 - k]
        else:
            source, target = c_send.at[k - 4], c_recv.at[7 - k]
        copy = pltpu.make_async_remote_copy(
            src_ref=source, dst_ref=target, send_sem=send_sem.at[k], recv_sem=recv_sem.at[k],
            device_id=device(*step), device_id_type=MESH,
        )
        copy.start()
        copies.append(copy)
    for copy in copies:
        copy.wait()


def finish_kernel(
    x_hi, x_lo, y_recv, z_recv, c_recv,
    y_low, y_high, w1, w2, w1c, w2c, p_low, p_high,
    fine_hbm, coarse_hbm,
    fine, coarse, level, zh_low, zh_high, sem,
):
    def stacked(hi, lo, tiles):
        thi, tlo = split(tiles)
        return jnp.concatenate([hi, thi, lo, tlo, hi, thi], 0)

    lane = lax.broadcasted_iota(jnp.int32, (1, 128), 1)
    for group in range(3):
        blocks = []
        for side in range(2):
            hi, lo = split(z_recv[side, 64 * group : 64 * group + 64])
            at = 8 * (group // 2)
            tiles = jnp.concatenate([c_recv[side, at : at + 8], c_recv[2 + side, at : at + 8]], 0)
            blocks += split(dot(y_low[group % 2], stacked(hi, lo, tiles)))
        both = jnp.concatenate(blocks, 1)
        if group < 2:
            for g in range(8):
                mask = jnp.where(lane // 16 == g, 1.0, 0.0).astype(BF16)
                mask = jnp.concatenate([mask] * 4, 1)
                zh_low[8 * group + g] = dot(both * mask, p_low[...]).astype(BF16)
        else:
            for g in range(16):
                mask = jnp.where(lane // 8 == g, 1.0, 0.0).astype(BF16)
                mask = jnp.concatenate([mask] * 4, 1)
                zh_high[g] = dot(both[:64] * mask, p_high[...]).astype(BF16)

    def write(bands, first, count, slot):
        src = fine.at[bands, pl.ds(first, count)]
        dst = fine_hbm.at[bands, pl.ds(first, count)]
        return pltpu.make_async_copy(src, dst, sem.at[slot])

    def lifted(x, table, tile_at):
        tiles = jnp.concatenate([y_recv[0, tile_at], y_recv[1, tile_at]], 0)
        return split(dot(table, stacked(x_hi[x], x_lo[x], tiles)))

    def low_four(q, carry):
        for i in range(4):
            x = 4 * q + i
            at = pl.ds(pl.multiple_of(16 * q + 8 * (i // 2), 8), 8)
            hi, lo = lifted(x, y_low[i % 2], at)
            extra = zh_low[q]
            one = dot(jnp.concatenate([hi[:64], lo[:64]], 1), w1[...])
            one = one + dot(jnp.concatenate([hi[:64], extra[:64]], 1), w2[i])
            fine[0, x] = one[:32, 128:192]
            fine[1, x] = one[32:, :64]
            fine[2, x] = one[32:, 128:192]
            two = dot(jnp.concatenate([hi[64:], lo[64:]], 1), w1c[...])
            level[x] = two + dot(jnp.concatenate([hi[64:], extra[64:]], 1), w2c[i])
        return carry

    def high_four(q, carry):
        for i in range(4):
            x = 4 * q + i
            at = pl.ds(pl.multiple_of(LOW_ROWS + 8 * q, 8), 8)
            hi, lo = lifted(HX + x, y_high[i], at)
            one = dot(jnp.concatenate([hi, lo], 1), w1[...])
            one = one + dot(jnp.concatenate([hi, zh_high[q]], 1), w2[i])
            fine[3, x] = one[:32, :64]
            fine[4, x] = one[:32, 128:192]
            fine[5, x] = one[32:, :64]
            fine[6, x] = one[32:, 128:192]
        return carry

    copies = []
    for part in range(4):
        lax.fori_loop(4 * part, 4 * part + 4, low_four, 0)
        copies.append(write(slice(0, 3), 16 * part, 16, part))
        copies[-1].start()

    def store(n, low, high):
        for bx, value in enumerate((low, high)):
            for by in range(2):
                for bz in range(2):
                    coarse[4 * bx + 2 * by + bz, n] = value[
                        16 * by : 16 * by + 16, 32 * bz : 32 * bz + 32
                    ]

    lift_loop(HX // 2, 2, lambda i: level[i], store)
    copies.append(pltpu.make_async_copy(coarse, coarse_hbm, sem.at[8]))
    copies[-1].start()
    for part in range(4):
        lax.fori_loop(4 * part, 4 * part + 4, high_four, 0)
        copies.append(write(slice(3, 7), 16 * part, 16, 4 + part))
        copies[-1].start()
    for copy in copies:
        copy.wait()


def body(velocity):
    send, work = constants()
    vmem = pl.BlockSpec(memory_space=pltpu.VMEM)
    hbm = pl.BlockSpec(memory_space=pl.ANY)
    shape = jax.ShapeDtypeStruct
    y_shape, z_shape, c_shape = (2, LOW_ROWS + HIGH_ROWS, BZ), (2, 3 * BY, 128), (4, 16, 128)
    halos = pl.pallas_call(
        exchange_kernel,
        out_shape=(
            shape((NX, BY, BZ), BF16), shape((NX, BY, BZ), BF16),
            shape(y_shape, F32), shape(z_shape, F32), shape(c_shape, F32),
        ),
        in_specs=[hbm] + [vmem] * 4,
        out_specs=(vmem,) * 5,
        scratch_shapes=[
            pltpu.VMEM((NX, BY, BZ), F32),
            pltpu.VMEM(y_shape, F32),
            pltpu.VMEM(z_shape, F32),
            pltpu.VMEM(c_shape, F32),
            pltpu.SemaphoreType.DMA((4,)),
            pltpu.SemaphoreType.DMA((8,)),
            pltpu.SemaphoreType.DMA((8,)),
        ],
        compiler_params=pltpu.CompilerParams(
            collective_id=0, has_side_effects=True, vmem_limit_bytes=24 * 2**20
        ),
        name="exchange",
    )(velocity, *[jnp.asarray(a) for a in send])
    fine_shape, coarse_shape = (7, HX, BY // 2, BZ // 2), (8, HX // 2, BY // 4, BZ // 4)
    return pl.pallas_call(
        finish_kernel,
        out_shape=(shape(fine_shape, F32), shape(coarse_shape, F32)),
        in_specs=[vmem] * 13,
        out_specs=(hbm, hbm),
        scratch_shapes=[
            pltpu.VMEM(fine_shape, F32),
            pltpu.VMEM(coarse_shape, F32),
            pltpu.VMEM((HX, 32, 128), F32),
            pltpu.VMEM((16, 96, 128), BF16),
            pltpu.VMEM((16, 64, 128), BF16),
            pltpu.SemaphoreType.DMA((9,)),
        ],
        compiler_params=pltpu.CompilerParams(vmem_limit_bytes=28 * 2**20),
        name="finish",
    )(*halos, *[jnp.asarray(a) for a in work])


def solution(mesh):
    return jax.shard_map(
        body,
        mesh=mesh,
        in_specs=(P(None, "gy", "gz"),),
        out_specs=(P(None, None, "gy", "gz"), P(None, None, "gy", "gz")),
        check_vma=False,
    )
```

```python
import functools

import jax
import jax.numpy as jnp
import ml_dtypes
import numpy as np
from jax import lax
from jax.experimental import pallas as pl
from jax.experimental.pallas import tpu as pltpu
from jax.sharding import PartitionSpec as P

predict_one = -1.586134342
update_one = -0.05298011854
predict_two = 0.8829110762
update_two = 0.4435068522
scale_factor = 1.149604398

MESH = pl.DeviceIdType.MESH
F32 = jnp.float32
BF16 = jnp.bfloat16
NX, HX = 128, 64
BY, BZ = 64, 128
LOW_ROWS, HIGH_ROWS = 4 * HX, 2 * HX


def lift_rows(v):
    s, d = v[0::2], v[1::2]
    d = d + predict_one * (s + np.roll(s, -1, 0))
    s = s + update_one * (np.roll(d, 1, 0) + d)
    d = d + predict_two * (s + np.roll(s, -1, 0))
    s = s + update_two * (np.roll(d, 1, 0) + d)
    return s * scale_factor, d / scale_factor


def factored(block, fine):
    first = np.linalg.svd(block[:fine])[2][:2]
    rest = block[fine:] - (block[fine:] @ first.T) @ first
    second = np.linalg.svd(rest)[2][:2]
    basis = np.concatenate([first, second])
    gains = block @ basis.T
    gains[:fine, 2:] = 0
    return basis, gains


@functools.cache
def operators(n):
    low, high = lift_rows(np.eye(3 * n))
    low2, high2 = lift_rows(low)
    h, q = n // 2, n // 4
    rows = np.concatenate([low[h : 2 * h], high[h : 2 * h], low2[q : 2 * q], high2[q : 2 * q]])
    return rows[:, n : 2 * n], factored(rows[:, :n], n), factored(rows[:, 2 * n :], n)


def halves(w):
    hi = w.astype(ml_dtypes.bfloat16)
    return hi, (w - hi.astype(np.float64)).astype(ml_dtypes.bfloat16)


def three(w, axis):
    hi, lo = halves(w)
    return np.concatenate([hi, hi, lo], axis)


@functools.cache
def constants():
    own_y, (basis_left, gain_left), (basis_right, gain_right) = operators(BY)
    y_low = np.zeros((2, 96, 80))
    y_high = np.zeros((4, 64, 80))
    for p in range(2):
        y_low[p, :, :64] = own_y
        y_low[p, :, 64 + 4 * p : 68 + 4 * p] = gain_left
        y_low[p, :, 72 + 4 * p : 76 + 4 * p] = gain_right
    for p in range(4):
        y_high[p, :, :64] = own_y[:64]
        y_high[p, :, 64 + 2 * p : 66 + 2 * p] = gain_left[:64, :2]
        y_high[p, :, 72 + 2 * p : 74 + 2 * p] = gain_right[:64, :2]
    edge = np.r_[0:16, 48:64]
    assert abs(np.delete(basis_left, edge, 1)).max() < 1e-12
    assert abs(np.delete(basis_right, edge, 1)).max() < 1e-12
    state_low = np.zeros((64, 256))
    state_high = np.zeros((32, 256))
    for side, basis in enumerate((basis_right, basis_left)):
        for i in range(8):
            columns = slice(32 * i, 32 * i + 32)
            state_low[32 * side + 4 * i : 32 * side + 4 * i + 4, columns] = basis[:, edge]
            state_high[16 * side + 2 * i : 16 * side + 2 * i + 2, columns] = basis[:2, edge]

    own_z, (left, gain_l), (right, gain_r) = operators(BZ)
    zs_low = np.concatenate([np.tile(b.T, (1, 16)) for b in (right, left)], 1)
    zs_high = np.concatenate([np.tile(b[:2].T, (1, 32)) for b in (right, left)], 1)

    def spread(rows):
        k = rows.shape[1]
        fine = np.zeros((k, 256))
        fine[:, :64] = rows[:64].T
        fine[:, 128:192] = rows[64:128].T
        coarse = np.zeros((k, 128))
        coarse[:, :64] = rows[128:].T
        return fine, coarse

    main_fine, main_coarse = spread(own_z)
    halo_fine, halo_coarse = spread(np.concatenate([gain_l, gain_r], 1))

    def passes(main, halo):
        hi, lo = halves(main)
        ehi, elo = halves(halo)
        table = np.zeros((4, 512, main.shape[1]), ml_dtypes.bfloat16)
        for i in range(4):
            table[i, :384] = np.concatenate([hi, hi, lo], 0)
            table[i, 384 + 32 * i : 384 + 32 * i + 24] = np.concatenate([ehi, ehi, elo], 0)
        return table

    def places(states):
        p = np.zeros((4, 128, 128))
        for lane in range(128):
            i, s = lane // states % 4, lane % states
            p[0, lane, 32 * i + s] = p[0, lane, 32 * i + 16 + s] = 1
            p[1, lane, 32 * i + 8 + s] = 1
            p[2, lane, 32 * i + 4 + s] = p[2, lane, 32 * i + 20 + s] = 1
            p[3, lane, 32 * i + 12 + s] = 1
        return p.reshape(512, 128).astype(ml_dtypes.bfloat16)

    wf, wc = passes(main_fine, halo_fine), passes(main_coarse, halo_coarse)
    y_low, y_high = three(y_low, 2), three(y_high, 2)
    send = (three(state_low, 1), three(state_high, 1), three(zs_low, 0), three(zs_high, 0), y_low, y_high)
    work = (y_low, wf, wc, places(4), places(2))
    return send, work


def split(v):
    hi = v.astype(BF16)
    return hi, (v - hi.astype(F32)).astype(BF16)


def dot(a, b):
    return jnp.dot(a, b, preferred_element_type=F32)


def lift_loop(count, unroll, load, store):
    k = 2 * count
    s_a, d_a, s_b, d_b, s_c, d_c, s_d = [load(i % k) for i in range(k - 4, k + 3)]
    d_a = d_a + predict_one * (s_a + s_b)
    d_b = d_b + predict_one * (s_b + s_c)
    s_b = s_b + update_one * (d_a + d_b)
    d_c = d_c + predict_one * (s_c + s_d)
    s_c = s_c + update_one * (d_b + d_c)
    d_b = d_b + predict_two * (s_b + s_c)

    def step(j, carry):
        s_now, d_before, s_before, d_done = carry
        for u in range(unroll):
            n = unroll * j + u + 1
            d_now, s_next = load(lax.rem(2 * n + 1, k)), load(lax.rem(2 * n + 2, k))
            d_now = d_now + predict_one * (s_now + s_next)
            s_now = s_now + update_one * (d_before + d_now)
            d_before = d_before + predict_two * (s_before + s_now)
            s_before = s_before + update_two * (d_done + d_before)
            store(n - 1, s_before * scale_factor, d_before * (1.0 / scale_factor))
            s_now, d_before, s_before, d_done = s_next, d_now, s_now, d_before
        return s_now, d_before, s_before, d_done

    lax.fori_loop(0, count // unroll, step, (s_d, d_c, s_c, d_b))


def lift_x(v, x_hi, x_lo, rows):
    def store(n, low, high):
        x_hi[n, rows], x_lo[n, rows] = split(low)
        x_hi[HX + n, rows], x_lo[HX + n, rows] = split(high)

    lift_loop(HX, 4, lambda i: v[i, rows], store)


def find_y_states(x_hi, x_lo, st_low, st_high, y_send):
    for half, table, per in ((0, st_low, 4), (1, st_high, 2)):
        n = 8 * per
        for g in range(0, 8, 2):
            columns = []
            for u in (g, g + 1):
                parts = []
                for ref in (x_hi, x_lo):
                    for x in range(HX * half + 8 * u, HX * half + 8 * u + 8):
                        parts += [ref[x, 0:16], ref[x, 48:64]]
                columns.append(jnp.concatenate(parts + parts[:16], 0))
            states = dot(table[...], jnp.concatenate(columns, 1))
            for u in (0, 1):
                at = LOW_ROWS * half + n * (g + u)
                for side in (0, 1):
                    piece = states[n * side : n * side + n, 128 * u : 128 * u + 128]
                    y_send[side, at : at + n] = piece


def find_z_states(x_hi, x_lo, zs_low, zs_high, z_send):
    lane = lax.broadcasted_iota(jnp.int32, (8, 128), 1)
    lower = (lane < 64)[None]
    for group, (first, count, table, per) in enumerate(
        ((0, 32, zs_low, 4), (32, 32, zs_low, 4), (64, 64, zs_high, 2))
    ):
        slot = lane % 64 // per
        n = count // 2
        both = []
        for at in (first, first + n):
            hi = x_hi[at : at + n].reshape(n * BY, BZ)
            lo = x_lo[at : at + n].reshape(n * BY, BZ)
            states = dot(jnp.concatenate([hi, lo, hi], 1), table[...]).reshape(n, 8, 8, 128)
            acc = states[0]
            for i in range(1, n):
                acc = jnp.where((slot == i)[None], states[i], acc)
            both.append(acc)
        one, two = both
        rows = slice(64 * group, 64 * group + 64)
        z_send[0, rows] = jnp.where(lower, one, pltpu.roll(two, 64, 2)).reshape(64, 128)
        z_send[1, rows] = jnp.where(lower, pltpu.roll(one, 64, 2), two).reshape(64, 128)


def find_corners(z_send, st_low, c_send):
    his, los = [], []
    zeros = jnp.zeros((32, 128), F32)
    for side in range(2):
        for group in range(4):
            if group == 3:
                piece = zeros
            else:
                at = 64 * group
                piece = jnp.concatenate(
                    [z_send[side, at : at + 16], z_send[side, at + 48 : at + 64]], 0
                )
            hi, lo = split(piece)
            his.append(hi)
            los.append(lo)
    c_send[...] = dot(st_low[...], jnp.concatenate(his + los + his, 0)).reshape(4, 16, 128)


STEPS = [(-1, 0), (1, 0), (0, -1), (0, 1), (-1, -1), (-1, 1), (1, -1), (1, 1)]
ORDER = (0, 3, 1, 2)


def exchange_kernel(
    v_hbm, st_low_hbm, st_high_hbm, zs_low_hbm, zs_high_hbm, y_low_hbm, y_high_hbm,
    lhs_low, lhs_high, z_recv, c_recv,
    v, x_hi, x_lo, y_send, z_send, c_send, y_recv,
    st_low, st_high, zs_low, zs_high, y_low, y_high, in_sem, send_sem, recv_sem,
):
    my_y, my_z = lax.axis_index("gy"), lax.axis_index("gz")
    n_y, n_z = lax.axis_size("gy"), lax.axis_size("gz")

    def device(step_y, step_z):
        return {
            "gy": lax.rem(my_y + step_y + n_y, n_y),
            "gz": lax.rem(my_z + step_z + n_z, n_z),
        }

    barrier = pltpu.get_barrier_semaphore()
    for step in STEPS:
        pl.semaphore_signal(barrier, inc=1, device_id=device(*step), device_id_type=MESH)

    def load(k, src, dst):
        copy = pltpu.make_async_copy(src, dst, in_sem.at[k])
        copy.start()
        return copy

    def load_rows(c):
        rows = pl.ds(16 * c, 16)
        return load(c, v_hbm.at[:, rows], v.at[:, rows])

    loads = {c: load_rows(c) for c in ORDER[:2]}
    loads[4] = load(4, st_low_hbm, st_low)
    loads[5] = load(5, st_high_hbm, st_high)
    loads.update({c: load_rows(c) for c in ORDER[2:]})
    loads[6] = load(6, zs_low_hbm, zs_low)
    loads[7] = load(7, zs_high_hbm, zs_high)
    loads[8] = load(8, y_low_hbm, y_low)
    loads[9] = load(9, y_high_hbm, y_high)

    def lift(c):
        loads[c].wait()
        lift_x(v, x_hi, x_lo, pl.ds(16 * c, 16))

    def send(k):
        source = (y_send, z_send, c_send)[k // 2 if k < 4 else 2]
        target = (y_recv, z_recv, c_recv)[k // 2 if k < 4 else 2]
        at, to = (k % 2, 1 - k % 2) if k < 4 else (k - 4, 7 - k)
        copy = pltpu.make_async_remote_copy(
            src_ref=source.at[at], dst_ref=target.at[to],
            send_sem=send_sem.at[k], recv_sem=recv_sem.at[k],
            device_id=device(*STEPS[k]), device_id_type=MESH,
        )
        copy.start()
        return copy

    lift(ORDER[0])
    lift(ORDER[1])
    loads[4].wait()
    loads[5].wait()
    find_y_states(x_hi, x_lo, st_low, st_high, y_send)
    pl.semaphore_wait(barrier, 8)
    y_copies = [send(k) for k in (0, 1)]

    lift(ORDER[2])
    lift(ORDER[3])
    loads[6].wait()
    loads[7].wait()
    find_z_states(x_hi, x_lo, zs_low, zs_high, z_send)
    z_copies = [send(k) for k in (2, 3)]
    find_corners(z_send, st_low, c_send)
    z_copies += [send(k) for k in range(4, 8)]

    loads[8].wait()
    loads[9].wait()
    for copy in y_copies:
        copy.wait()
    for part in range(4):
        lift_y(part, True, x_hi, x_lo, y_recv, y_low, lhs_low)
        lift_y(part, False, x_hi, x_lo, y_recv, y_high, lhs_high)
    for copy in z_copies:
        copy.wait()


def stacked(hi, lo, tiles):
    thi, tlo = split(tiles)
    return jnp.concatenate([hi, thi, lo, tlo, hi, thi], 0)


def lift_z_halos(z_recv, c_recv, y_low, p_low, p_high, zh_low, zh_high):
    lane = lax.broadcasted_iota(jnp.int32, (1, 512), 1) % 128
    for group in range(3):
        blocks = []
        for side in range(2):
            hi, lo = split(z_recv[side, 64 * group : 64 * group + 64])
            at = 8 * (group // 2)
            tiles = jnp.concatenate([c_recv[side, at : at + 8], c_recv[2 + side, at : at + 8]], 0)
            blocks += split(dot(y_low[group % 2], stacked(hi, lo, tiles)))
        both = jnp.concatenate(blocks, 1)
        if group < 2:
            masked = [both * jnp.where(lane // 16 == g, 1.0, 0.0).astype(BF16) for g in range(8)]
            placed = dot(jnp.concatenate(masked, 0), p_low[...]).astype(BF16)
            zh_low[8 * group : 8 * group + 8] = placed.reshape(8, 96, 128)
        else:
            both = both[:64]
            masked = [both * jnp.where(lane // 8 == g, 1.0, 0.0).astype(BF16) for g in range(16)]
            placed = dot(jnp.concatenate(masked, 0), p_high[...]).astype(BF16)
            zh_high[...] = placed.reshape(16, 64, 128)


def lift_y(part, low, x_hi, x_lo, y_recv, table, lhs):
    first = 0 if low else HX
    for i in range(4):
        for q in range(0, 4, 2):
            columns = []
            for u in (q, q + 1):
                x = 16 * part + 4 * u + i
                at = 8 * (x // 2) if low else LOW_ROWS + 8 * (x // 4)
                tiles = jnp.concatenate([y_recv[0, at : at + 8], y_recv[1, at : at + 8]], 0)
                columns.append(stacked(x_hi[first + x], x_lo[first + x], tiles))
            which = i % 2 if low else i
            hi, lo = split(dot(table[which], jnp.concatenate(columns, 1)))
            for u in (0, 1):
                lhs[0, part, i, q + u] = hi[:, 128 * u : 128 * u + 128]
                lhs[1, part, i, q + u] = lo[:, 128 * u : 128 * u + 128]


def lift_z(part, i, zh, lhs, table, start, rows):
    hi = lhs[0, part, i, :, start : start + rows].reshape(4 * rows, 128)
    lo = lhs[1, part, i, :, start : start + rows].reshape(4 * rows, 128)
    zh = zh[4 * part : 4 * part + 4, start : start + rows].reshape(4 * rows, 128)
    return dot(jnp.concatenate([hi, lo, hi, zh], 1), table[i])


def low_part(part, lhs, zh_low, wf, wc, fine, level):
    for i in range(4):
        one = lift_z(part, i, zh_low, lhs, wf, 0, 64)
        two = lift_z(part, i, zh_low, lhs, wc, 64, 32)
        for q in range(4):
            x = 16 * part + 4 * q + i
            fine[0, x] = one[64 * q : 64 * q + 32, 128:192]
            fine[1, x] = one[64 * q + 32 : 64 * q + 64, :64]
            fine[2, x] = one[64 * q + 32 : 64 * q + 64, 128:192]
            level[x] = two[32 * q : 32 * q + 32]


def high_part(part, lhs, zh_high, wf, fine):
    for i in range(4):
        one = lift_z(part, i, zh_high, lhs, wf, 0, 64)
        for q in range(4):
            x = 16 * part + 4 * q + i
            fine[3, x] = one[64 * q : 64 * q + 32, :64]
            fine[4, x] = one[64 * q : 64 * q + 32, 128:192]
            fine[5, x] = one[64 * q + 32 : 64 * q + 64, :64]
            fine[6, x] = one[64 * q + 32 : 64 * q + 64, 128:192]


def lift_level(level, coarse):
    def store(n, low, high):
        for bx, value in enumerate((low, high)):
            for by in range(2):
                for bz in range(2):
                    coarse[4 * bx + 2 * by + bz, n] = value[
                        16 * by : 16 * by + 16, 32 * bz : 32 * bz + 32
                    ]

    lift_loop(HX // 2, 8, lambda i: level[i], store)


def finish_kernel(
    lhs_low, lhs_high, z_recv, c_recv, y_low, wf, wc, p_low, p_high,
    fine_hbm, coarse_hbm,
    fine, coarse, level, zh_low, zh_high, sem,
):
    lift_z_halos(z_recv, c_recv, y_low, p_low, p_high, zh_low, zh_high)
    copies = []

    def write(bands, part):
        at = pl.ds(16 * part, 16)
        src, dst = fine.at[pl.ds(*bands), at], fine_hbm.at[pl.ds(*bands), at]
        copies.append(pltpu.make_async_copy(src, dst, sem.at[part + (4 if bands == HIGH_BANDS else 0)]))
        copies[-1].start()

    for part in range(4):
        low_part(part, lhs_low, zh_low, wf, wc, fine, level)
        write(LOW_BANDS, part)
    lift_level(level, coarse)
    copies.append(pltpu.make_async_copy(coarse, coarse_hbm, sem.at[8]))
    copies[-1].start()
    for part in range(4):
        high_part(part, lhs_high, zh_high, wf, fine)
        write(HIGH_BANDS, part)
    for copy in copies:
        copy.wait()


LOW_BANDS, HIGH_BANDS = (0, 3), (3, 4)


def body(velocity):
    send, work = constants()
    vmem = pl.BlockSpec(memory_space=pltpu.VMEM)
    hbm = pl.BlockSpec(memory_space=pltpu.HBM)
    shape = jax.ShapeDtypeStruct
    y_shape, z_shape, c_shape = (2, LOW_ROWS + HIGH_ROWS, BZ), (2, 3 * BY, 128), (4, 16, 128)
    halos = pl.pallas_call(
        exchange_kernel,
        out_shape=(
            shape((2, 4, 4, 4, 96, 128), BF16), shape((2, 4, 4, 4, 64, 128), BF16),
            shape(z_shape, F32), shape(c_shape, F32),
        ),
        in_specs=[hbm] * 7,
        out_specs=(vmem,) * 4,
        scratch_shapes=[
            pltpu.VMEM((NX, BY, BZ), F32),
            pltpu.VMEM((NX, BY, BZ), BF16),
            pltpu.VMEM((NX, BY, BZ), BF16),
            pltpu.VMEM(y_shape, F32),
            pltpu.VMEM(z_shape, F32),
            pltpu.VMEM(c_shape, F32),
            pltpu.VMEM(y_shape, F32),
            *[pltpu.VMEM(a.shape, BF16) for a in send],
            pltpu.SemaphoreType.DMA((10,)),
            pltpu.SemaphoreType.DMA((8,)),
            pltpu.SemaphoreType.DMA((8,)),
        ],
        compiler_params=pltpu.CompilerParams(
            collective_id=0, has_side_effects=True, vmem_limit_bytes=32 * 2**20
        ),
        name="exchange",
    )(*[pltpu.with_memory_space_constraint(jnp.asarray(a), pltpu.HBM) for a in (velocity, *send)])
    fine_shape, coarse_shape = (7, HX, BY // 2, BZ // 2), (8, HX // 2, BY // 4, BZ // 4)
    return pl.pallas_call(
        finish_kernel,
        out_shape=(shape(fine_shape, F32), shape(coarse_shape, F32)),
        in_specs=[vmem] * 9,
        out_specs=(hbm, hbm),
        scratch_shapes=[
            pltpu.VMEM(fine_shape, F32),
            pltpu.VMEM(coarse_shape, F32),
            pltpu.VMEM((HX, 32, 128), F32),
            pltpu.VMEM((16, 96, 128), BF16),
            pltpu.VMEM((16, 64, 128), BF16),
            pltpu.SemaphoreType.DMA((9,)),
        ],
        compiler_params=pltpu.CompilerParams(vmem_limit_bytes=28 * 2**20),
        name="finish",
    )(*halos, *[jnp.asarray(a) for a in work])


def solution(mesh):
    return jax.shard_map(
        body,
        mesh=mesh,
        in_specs=(P(None, "gy", "gz"),),
        out_specs=(P(None, None, "gy", "gz"), P(None, None, "gy", "gz")),
        check_vma=False,
    )
```

```python
import functools

import jax
import jax.numpy as jnp
import ml_dtypes
import numpy as np
from jax import lax
from jax.experimental import pallas as pl
from jax.experimental.pallas import tpu as pltpu
from jax.sharding import PartitionSpec as P

predict_one = -1.586134342
update_one = -0.05298011854
predict_two = 0.8829110762
update_two = 0.4435068522
scale_factor = 1.149604398

MESH = pl.DeviceIdType.MESH
F32 = jnp.float32
BF16 = jnp.bfloat16
NX, HX = 128, 64
BY, BZ = 64, 128
Y_ROWS = 2 * NX + HX
Z_ROWS = 2 * BY + BY // 2


def lift_rows(v):
    s, d = v[0::2], v[1::2]
    d = d + predict_one * (s + np.roll(s, -1, 0))
    s = s + update_one * (np.roll(d, 1, 0) + d)
    d = d + predict_two * (s + np.roll(s, -1, 0))
    s = s + update_two * (np.roll(d, 1, 0) + d)
    return s * scale_factor, d / scale_factor


def factored(block, fine):
    first = np.linalg.svd(block[:fine])[2][:2]
    rest = block[fine:] - (block[fine:] @ first.T) @ first
    second = np.linalg.svd(rest)[2][:2]
    basis = np.concatenate([first, second])
    gains = block @ basis.T
    gains[:fine, 2:] = 0
    return basis, gains


@functools.cache
def operators(n):
    low, high = lift_rows(np.eye(3 * n))
    low2, high2 = lift_rows(low)
    h, q = n // 2, n // 4
    rows = np.concatenate([low[h : 2 * h], high[h : 2 * h], low2[q : 2 * q], high2[q : 2 * q]])
    return rows[:, n : 2 * n], factored(rows[:, :n], n), factored(rows[:, 2 * n :], n)


def halves(w):
    hi = w.astype(ml_dtypes.bfloat16)
    return hi, (w - hi.astype(np.float64)).astype(ml_dtypes.bfloat16)


def three(w, axis):
    hi, lo = halves(w)
    return np.concatenate([hi, hi, lo], axis)


@functools.cache
def constants():
    own_y, (basis_left, gain_left), (basis_right, gain_right) = operators(BY)
    y_low = np.zeros((4, 96, 80))
    for p in range(4):
        y_low[p, :, :64] = own_y
        y_low[p, :, 64 + 2 * p : 66 + 2 * p] = gain_left[:, :2]
        y_low[p, :, 72 + 2 * p : 74 + 2 * p] = gain_right[:, :2]
    y_high = y_low[:, :64]
    y_more = np.zeros((4, 32, 16))
    for p in range(4):
        y_more[p, :, 2 * p : 2 * p + 2] = gain_left[64:, 2:]
        y_more[p, :, 8 + 2 * p : 10 + 2 * p] = gain_right[64:, 2:]
    corner = np.zeros((2, 96, 32))
    for group in range(2):
        for side, gain in enumerate((gain_left, gain_right)):
            for p in range(2):
                at = 16 * p + 8 * side + 2 * group
                corner[group, :, at : at + 2] = gain[:, 2 * p : 2 * p + 2]
    z_one = np.concatenate([own_y, corner[0]], 1)
    z_two = corner[1, 64:]
    coarse_y = own_y[64:]
    edge = np.r_[0:16, 48:64]
    assert abs(np.delete(basis_left, edge, 1)).max() < 1e-12
    assert abs(np.delete(basis_right, edge, 1)).max() < 1e-12
    state_low = np.zeros((64, 256))
    state_high = np.zeros((32, 256))
    for side, basis in enumerate((basis_right, basis_left)):
        for i in range(8):
            columns = slice(32 * i, 32 * i + 32)
            for p in range(2):
                at = 32 * side + 16 * p + 2 * i
                state_low[at : at + 2, columns] = basis[2 * p : 2 * p + 2, edge]
            state_high[16 * side + 2 * i : 16 * side + 2 * i + 2, columns] = basis[:2, edge]

    own_z, (left, gain_l), (right, gain_r) = operators(BZ)
    zs_low = np.concatenate([np.tile(b[p : p + 2].T, (1, 16)) for b in (right, left) for p in (0, 2)], 1)
    zs_high = np.concatenate([np.tile(b[:2].T, (1, 32)) for b in (right, left)], 1)
    coarse_z = np.zeros((2, 384, 128), ml_dtypes.bfloat16)
    for p in range(2):
        coarse_z[p, :, 64 * p : 64 * p + 64] = three(own_z[128:].T, 0)
    coarse_z = coarse_z.reshape(768, 128)

    def spread(rows):
        k = rows.shape[1]
        fine = np.zeros((k, 256))
        fine[:, :64] = rows[:64].T
        fine[:, 128:192] = rows[64:128].T
        coarse = np.zeros((k, 128))
        coarse[:, :64] = rows[128:].T
        return fine, coarse

    main_fine, main_coarse = spread(own_z)
    halo_fine, halo_coarse = spread(np.concatenate([gain_l, gain_r], 1))

    def passes(main, halo):
        hi, lo = halves(main)
        ehi, elo = halves(halo)
        table = np.zeros((4, 512, main.shape[1]), ml_dtypes.bfloat16)
        for i in range(4):
            table[i, :384] = np.concatenate([hi, hi, lo], 0)
            table[i, 384 + 32 * i : 384 + 32 * i + 24] = np.concatenate([ehi, ehi, elo], 0)
        return table

    def places(first):
        p = np.zeros((4, 128, 128))
        for lane in range(128):
            i, s = lane // 2 % 4, first + lane % 2
            p[0, lane, 32 * i + s] = p[0, lane, 32 * i + 16 + s] = 1
            p[1, lane, 32 * i + 8 + s] = 1
            p[2, lane, 32 * i + 4 + s] = p[2, lane, 32 * i + 20 + s] = 1
            p[3, lane, 32 * i + 12 + s] = 1
        return p.reshape(512, 128).astype(ml_dtypes.bfloat16)

    wf, wc = passes(main_fine, halo_fine), passes(main_coarse, halo_coarse)
    send = (
        three(state_low, 1), three(state_high, 1), three(zs_low, 0), three(zs_high, 0), coarse_z, three(coarse_y, 1),
        three(y_low, 2), three(y_high, 2), three(y_more, 2).reshape(128, 48),
    )
    work = (
        three(z_one, 1), three(z_two, 1), three(y_high[2], 1), wf, wc,
        np.concatenate([places(0), places(2)], 0),
    )
    return send, work


def split(v):
    hi = v.astype(BF16)
    return hi, (v - hi.astype(F32)).astype(BF16)


def dot(a, b):
    return jnp.dot(a, b, preferred_element_type=F32)


def lift_loop(count, unroll, load, store):
    k = 2 * count
    s_a, d_a, s_b, d_b, s_c, d_c, s_d = [load(i % k) for i in range(k - 4, k + 3)]
    d_a = d_a + predict_one * (s_a + s_b)
    d_b = d_b + predict_one * (s_b + s_c)
    s_b = s_b + update_one * (d_a + d_b)
    d_c = d_c + predict_one * (s_c + s_d)
    s_c = s_c + update_one * (d_b + d_c)
    d_b = d_b + predict_two * (s_b + s_c)

    def step(j, carry):
        s_now, d_before, s_before, d_done = carry
        for u in range(unroll):
            n = unroll * j + u + 1
            d_now, s_next = load(lax.rem(2 * n + 1, k)), load(lax.rem(2 * n + 2, k))
            d_now = d_now + predict_one * (s_now + s_next)
            s_now = s_now + update_one * (d_before + d_now)
            d_before = d_before + predict_two * (s_before + s_now)
            s_before = s_before + update_two * (d_done + d_before)
            store(n - 1, s_before * scale_factor, d_before * (1.0 / scale_factor))
            s_now, d_before, s_before, d_done = s_next, d_now, s_now, d_before
        return s_now, d_before, s_before, d_done

    lax.fori_loop(0, count // unroll, step, (s_d, d_c, s_c, d_b))


def lift_x(v, x_hi, x_lo, rows):
    def store(n, low, high):
        x_hi[n, rows], x_lo[n, rows] = split(low)
        x_hi[HX + n, rows], x_lo[HX + n, rows] = split(high)

    lift_loop(HX, 16, lambda i: v[i, rows], store)


def find_y_states(x_hi, x_lo, st_low, st_high, coarse_z, y_send):
    more = [[], []]
    for half, table in ((0, st_low), (1, st_high)):
        n = 16
        for g in range(0, 8, 2):
            columns = []
            for u in (g, g + 1):
                parts = []
                for ref in (x_hi, x_lo):
                    for x in range(HX * half + 8 * u, HX * half + 8 * u + 8):
                        parts += [ref[x, 0:16], ref[x, 48:64]]
                columns.append(jnp.concatenate(parts + parts[:16], 0))
            states = dot(table[...], jnp.concatenate(columns, 1))
            for u in (0, 1):
                at = NX * half + n * (g + u)
                for side in (0, 1):
                    first = (n if half else 2 * n) * side
                    lanes = slice(128 * u, 128 * u + 128)
                    y_send[side, at : at + n] = states[first : first + n, lanes]
                    if not half:
                        more[side].append(states[first + n : first + 2 * n, lanes])
    pieces = []
    for part in range(2):
        hi, lo = split(jnp.concatenate(more[0][4 * part : 4 * part + 4] + more[1][4 * part : 4 * part + 4], 0))
        pieces += [hi, lo, hi]
    lifted = dot(jnp.concatenate(pieces, 1), coarse_z[...])
    y_send[0, 2 * NX :] = lifted[:HX]
    y_send[1, 2 * NX :] = lifted[HX:]


def find_z_states(x_hi, x_lo, zs_low, zs_high, coarse_y, z_send, z_raw):
    lane = lax.broadcasted_iota(jnp.int32, (8, 128), 1)

    def states_of(first, n, table, slot):
        hi = x_hi[first : first + n].reshape(n * BY, BZ)
        lo = x_lo[first : first + n].reshape(n * BY, BZ)
        states = dot(jnp.concatenate([hi, lo, hi], 1), table[...]).reshape(n, 8, 8, 128)
        acc = states[0]
        for i in range(1, n):
            acc = jnp.where((slot == i)[None], states[i], acc)
        return acc

    def gathered(pieces, of):
        width = 128 // len(pieces)
        out = None
        for k, piece in enumerate(pieces):
            turn = (width * (k - of)) % 128
            moved = pltpu.roll(piece, turn, 2) if turn else piece
            out = moved if out is None else jnp.where((lane // width == k)[None], moved, out)
        return out.reshape(64, 128)

    low = [states_of(16 * k, 16, zs_low, lane % 32 // 2) for k in range(4)]
    high = [states_of(HX + 32 * k, 32, zs_high, lane % 64 // 2) for k in range(2)]
    columns = []
    for side in range(2):
        z_send[side, 0:64] = gathered(low, 2 * side)
        z_send[side, 64:128] = gathered(high, side)
        second = gathered(low, 2 * side + 1)
        z_raw[side] = second
        hi, lo = split(second)
        columns.append(jnp.concatenate([hi, lo, hi], 0))
    lifted = dot(coarse_y[...], jnp.concatenate(columns, 1))
    z_send[0, 128:160] = lifted[:, :128]
    z_send[1, 128:160] = lifted[:, 128:]


def find_corners(z_send, z_raw, st_low, c_send):
    his, los = [], []
    zeros = jnp.zeros((32, 128), F32)
    for side in range(2):
        for top, low in (
            (z_send[side, 0:16], z_send[side, 48:64]),
            (z_raw[side, 0:16], z_raw[side, 48:64]),
            (z_send[side, 64:80], z_send[side, 112:128]),
            (zeros[:16], zeros[:16]),
        ):
            hi, lo = split(jnp.concatenate([top, low], 0))
            his.append(hi)
            los.append(lo)
    states = dot(st_low[...], jnp.concatenate(his + los + his, 0))
    for y in range(2):
        for z in range(2):
            for p in range(2):
                at = 32 * y + 16 * p + 8 * z
                c_send[2 * y + z, 8 * p : 8 * p + 8] = states[at : at + 8]


STEPS = [(-1, 0), (1, 0), (0, -1), (0, 1), (-1, -1), (-1, 1), (1, -1), (1, 1)]
ORDER = (0, 3, 1, 2)


def exchange_kernel(
    v_hbm, st_low_hbm, st_high_hbm, zs_low_hbm, zs_high_hbm, coarse_z_hbm, coarse_y_hbm,
    y_low_hbm, y_high_hbm, y_more_hbm,
    lhs_low, lhs_high, more, z_recv, c_recv,
    v, x_hi, x_lo, y_send, z_send, z_raw, c_send, y_recv,
    st_low, st_high, zs_low, zs_high, coarse_z, coarse_y, y_low, y_high, y_more, in_sem, send_sem, recv_sem,
):
    my_y, my_z = lax.axis_index("gy"), lax.axis_index("gz")
    n_y, n_z = lax.axis_size("gy"), lax.axis_size("gz")

    def device(step_y, step_z):
        return {
            "gy": lax.rem(my_y + step_y + n_y, n_y),
            "gz": lax.rem(my_z + step_z + n_z, n_z),
        }

    barrier = pltpu.get_barrier_semaphore()
    for step in STEPS:
        pl.semaphore_signal(barrier, inc=1, device_id=device(*step), device_id_type=MESH)

    def load(k, src, dst):
        copy = pltpu.make_async_copy(src, dst, in_sem.at[k])
        copy.start()
        return copy

    def load_rows(c):
        rows = pl.ds(16 * c, 16)
        return load(c, v_hbm.at[:, rows], v.at[:, rows])

    loads = {c: load_rows(c) for c in ORDER[:2]}
    tables = [
        (st_low_hbm, st_low), (st_high_hbm, st_high), (coarse_z_hbm, coarse_z), (zs_low_hbm, zs_low),
        (zs_high_hbm, zs_high), (coarse_y_hbm, coarse_y), (y_low_hbm, y_low), (y_high_hbm, y_high), (y_more_hbm, y_more),
    ]
    for k in (0, 1, 2):
        loads[4 + k] = load(4 + k, *tables[k])
    loads.update({c: load_rows(c) for c in ORDER[2:]})
    for k in range(3, 9):
        loads[4 + k] = load(4 + k, *tables[k])

    def lift(c):
        loads[c].wait()
        lift_x(v, x_hi, x_lo, pl.ds(16 * c, 16))

    def send(k):
        source = (y_send, z_send, c_send)[k // 2 if k < 4 else 2]
        target = (y_recv, z_recv, c_recv)[k // 2 if k < 4 else 2]
        at, to = (k % 2, 1 - k % 2) if k < 4 else (k - 4, 7 - k)
        copy = pltpu.make_async_remote_copy(
            src_ref=source.at[at], dst_ref=target.at[to],
            send_sem=send_sem.at[k], recv_sem=recv_sem.at[k],
            device_id=device(*STEPS[k]), device_id_type=MESH,
        )
        copy.start()
        return copy

    lift(ORDER[0])
    lift(ORDER[1])
    for k in (4, 5, 6):
        loads[k].wait()
    find_y_states(x_hi, x_lo, st_low, st_high, coarse_z, y_send)
    pl.semaphore_wait(barrier, 8)
    y_copies = [send(k) for k in (0, 1)]

    lift(ORDER[2])
    lift(ORDER[3])
    for k in (7, 8, 9):
        loads[k].wait()
    find_z_states(x_hi, x_lo, zs_low, zs_high, coarse_y, z_send, z_raw)
    z_copies = [send(k) for k in (2, 3)]
    find_corners(z_send, z_raw, st_low, c_send)
    z_copies += [send(k) for k in range(4, 8)]

    for k in (10, 11, 12):
        loads[k].wait()
    for copy in y_copies:
        copy.wait()
    lift_more(y_recv, y_more, more)
    for part in range(4):
        lift_y(part, True, x_hi, x_lo, y_recv, y_low, lhs_low)
        lift_y(part, False, x_hi, x_lo, y_recv, y_high, lhs_high)
    for copy in z_copies:
        copy.wait()


def stacked(hi, lo, tiles):
    thi, tlo = split(tiles)
    return jnp.concatenate([hi, thi, lo, tlo, hi, thi], 0)


def lift_z_halos(z_recv, c_recv, z_one, z_two, z_high, places, zh_low, zh_high):
    lane = lax.broadcasted_iota(jnp.int32, (1, 512), 1) % 128
    masks = [jnp.where(lane // 8 == g, 1.0, 0.0).astype(BF16) for g in range(16)]
    first, second, high = [], [], []
    for side in range(2):
        corners = [c_recv[2 * y + side, 8 * p : 8 * p + 8] for p in range(2) for y in range(2)]
        tiles = jnp.concatenate(corners, 0)
        own = z_recv[side]
        first += split(dot(z_one[...], tripled(jnp.concatenate([own[:64], tiles], 0))))
        second += split(own[128:160] + dot(z_two[...], tripled(tiles)))
        high += split(dot(z_high[...], tripled(jnp.concatenate([own[64:128], tiles[:16]], 0))))
    first, second, high = (jnp.concatenate(blocks, 1) for blocks in (first, second, high))
    one = jnp.concatenate([high * m for m in masks], 0)
    zh_high[...] = dot(one, places[:512]).astype(BF16).reshape(16, 64, 128)
    one = jnp.concatenate([first[:64] * m for m in masks], 0)
    zh_low[:, :64] = dot(one, places[:512]).astype(BF16).reshape(16, 64, 128)
    both = [jnp.concatenate([first[64:] * m, second * m], 1) for m in masks]
    both = dot(jnp.concatenate(both, 0), places[...])
    zh_low[:, 64:] = both.astype(BF16).reshape(16, 32, 128)


def tripled(v):
    hi, lo = split(v)
    return jnp.concatenate([hi, lo, hi], 0)


def lift_more(y_recv, y_more, more):
    for t in range(0, 8, 2):
        columns = []
        for u in (t, t + 1):
            at = 2 * NX + 8 * u
            columns.append(tripled(jnp.concatenate([y_recv[0, at : at + 8], y_recv[1, at : at + 8]], 0)))
        lifted = dot(y_more[...], jnp.concatenate(columns, 1))
        for u in (0, 1):
            for i in range(4):
                value = lifted[32 * i : 32 * i + 32, 128 * u : 128 * u + 128]
                x = 4 * (t + u) + i
                more[x] = value
                more[HX // 2 + x] = pltpu.roll(value, 64, 1)


def lift_y(part, low, x_hi, x_lo, y_recv, table, lhs):
    first = 0 if low else HX
    for i in range(4):
        for q in range(0, 4, 2):
            columns = []
            for u in (q, q + 1):
                x = first + 16 * part + 4 * u + i
                at = 8 * (x // 4)
                tiles = jnp.concatenate([y_recv[0, at : at + 8], y_recv[1, at : at + 8]], 0)
                columns.append(stacked(x_hi[x], x_lo[x], tiles))
            hi, lo = split(dot(table[i], jnp.concatenate(columns, 1)))
            for u in (0, 1):
                lhs[0, part, i, q + u] = hi[:, 128 * u : 128 * u + 128]
                lhs[1, part, i, q + u] = lo[:, 128 * u : 128 * u + 128]


def lift_z(part, i, zh, lhs, table, start, rows):
    hi = lhs[0, part, i, :, start : start + rows].reshape(4 * rows, 128)
    lo = lhs[1, part, i, :, start : start + rows].reshape(4 * rows, 128)
    zh = zh[4 * part : 4 * part + 4, start : start + rows].reshape(4 * rows, 128)
    return dot(jnp.concatenate([hi, lo, hi, zh], 1), table[i])


def low_part(part, lhs, more, zh_low, wf, wc, fine, level):
    for i in range(4):
        one = lift_z(part, i, zh_low, lhs, wf, 0, 64)
        two = lift_z(part, i, zh_low, lhs, wc, 64, 32)
        for q in range(4):
            x = 16 * part + 4 * q + i
            fine[0, x] = one[64 * q : 64 * q + 32, 128:192]
            fine[1, x] = one[64 * q + 32 : 64 * q + 64, :64]
            fine[2, x] = one[64 * q + 32 : 64 * q + 64, 128:192]
            level[x] = two[32 * q : 32 * q + 32] + more[x]


def high_part(part, lhs, zh_high, wf, fine):
    for i in range(4):
        one = lift_z(part, i, zh_high, lhs, wf, 0, 64)
        for q in range(4):
            x = 16 * part + 4 * q + i
            fine[3, x] = one[64 * q : 64 * q + 32, :64]
            fine[4, x] = one[64 * q : 64 * q + 32, 128:192]
            fine[5, x] = one[64 * q + 32 : 64 * q + 64, :64]
            fine[6, x] = one[64 * q + 32 : 64 * q + 64, 128:192]


def lift_level(level, coarse):
    def store(n, low, high):
        for bx, value in enumerate((low, high)):
            for by in range(2):
                for bz in range(2):
                    coarse[4 * bx + 2 * by + bz, n] = value[
                        16 * by : 16 * by + 16, 32 * bz : 32 * bz + 32
                    ]

    lift_loop(HX // 2, 16, lambda i: level[i], store)


def finish_kernel(
    lhs_low, lhs_high, more, z_recv, c_recv, z_one, z_two, z_high, wf, wc, places,
    fine_hbm, coarse_hbm,
    fine, coarse, level, zh_low, zh_high, sem,
):
    copies = []

    def write(bands, part):
        at = pl.ds(16 * part, 16)
        src, dst = fine.at[pl.ds(*bands), at], fine_hbm.at[pl.ds(*bands), at]
        copies.append(pltpu.make_async_copy(src, dst, sem.at[part + (4 if bands == HIGH_BANDS else 0)]))
        copies[-1].start()

    lift_z_halos(z_recv, c_recv, z_one, z_two, z_high, places, zh_low, zh_high)
    for part in range(4):
        low_part(part, lhs_low, more, zh_low, wf, wc, fine, level)
        write(LOW_BANDS, part)
    lift_level(level, coarse)
    copies.append(pltpu.make_async_copy(coarse, coarse_hbm, sem.at[8]))
    copies[-1].start()
    for part in range(4):
        high_part(part, lhs_high, zh_high, wf, fine)
        write(HIGH_BANDS, part)
    for copy in copies:
        copy.wait()


LOW_BANDS, HIGH_BANDS = (0, 3), (3, 4)


def body(velocity):
    send, work = constants()
    vmem = pl.BlockSpec(memory_space=pltpu.VMEM)
    hbm = pl.BlockSpec(memory_space=pltpu.HBM)
    shape = jax.ShapeDtypeStruct
    y_shape, z_shape, c_shape = (2, Y_ROWS, BZ), (2, Z_ROWS, 128), (4, 16, 128)
    halos = pl.pallas_call(
        exchange_kernel,
        out_shape=(
            shape((2, 4, 4, 4, 96, 128), BF16), shape((2, 4, 4, 4, 64, 128), BF16),
            shape((HX, 32, 128), F32), shape(z_shape, F32), shape(c_shape, F32),
        ),
        in_specs=[hbm] * 10,
        out_specs=(vmem,) * 5,
        scratch_shapes=[
            pltpu.VMEM((NX, BY, BZ), F32),
            pltpu.VMEM((NX, BY, BZ), BF16),
            pltpu.VMEM((NX, BY, BZ), BF16),
            pltpu.VMEM(y_shape, F32),
            pltpu.VMEM(z_shape, F32),
            pltpu.VMEM((2, BY, 128), F32),
            pltpu.VMEM(c_shape, F32),
            pltpu.VMEM(y_shape, F32),
            *[pltpu.VMEM(a.shape, BF16) for a in send],
            pltpu.SemaphoreType.DMA((13,)),
            pltpu.SemaphoreType.DMA((8,)),
            pltpu.SemaphoreType.DMA((8,)),
        ],
        compiler_params=pltpu.CompilerParams(
            collective_id=0, has_side_effects=True, vmem_limit_bytes=32 * 2**20
        ),
        name="exchange",
    )(*[pltpu.with_memory_space_constraint(jnp.asarray(a), pltpu.HBM) for a in (velocity, *send)])
    fine_shape, coarse_shape = (7, HX, BY // 2, BZ // 2), (8, HX // 2, BY // 4, BZ // 4)
    return pl.pallas_call(
        finish_kernel,
        out_shape=(shape(fine_shape, F32), shape(coarse_shape, F32)),
        in_specs=[vmem] * 11,
        out_specs=(hbm, hbm),
        scratch_shapes=[
            pltpu.VMEM(fine_shape, F32),
            pltpu.VMEM(coarse_shape, F32),
            pltpu.VMEM((HX, 32, 128), F32),
            pltpu.VMEM((16, 96, 128), BF16),
            pltpu.VMEM((16, 64, 128), BF16),
            pltpu.SemaphoreType.DMA((9,)),
        ],
        compiler_params=pltpu.CompilerParams(vmem_limit_bytes=28 * 2**20),
        name="finish",
    )(*halos, *[jnp.asarray(a) for a in work])


def solution(mesh):
    return jax.shard_map(
        body,
        mesh=mesh,
        in_specs=(P(None, "gy", "gz"),),
        out_specs=(P(None, None, "gy", "gz"), P(None, None, "gy", "gz")),
        check_vma=False,
    )
```

```python
import functools

import jax
import jax.numpy as jnp
import ml_dtypes
import numpy as np
from jax import lax
from jax.experimental import pallas as pl
from jax.experimental.pallas import tpu as pltpu
from jax.sharding import PartitionSpec as P

predict_one = -1.586134342
update_one = -0.05298011854
predict_two = 0.8829110762
update_two = 0.4435068522
scale_factor = 1.149604398

MESH = pl.DeviceIdType.MESH
F32 = jnp.float32
BF16 = jnp.bfloat16
NX, HX = 128, 64
BY, BZ = 64, 128
Y_ROWS = 2 * NX + HX
Z_ROWS = 2 * BY + BY // 2


def lift_rows(v):
    s, d = v[0::2], v[1::2]
    d = d + predict_one * (s + np.roll(s, -1, 0))
    s = s + update_one * (np.roll(d, 1, 0) + d)
    d = d + predict_two * (s + np.roll(s, -1, 0))
    s = s + update_two * (np.roll(d, 1, 0) + d)
    return s * scale_factor, d / scale_factor


def factored(block, fine):
    first = np.linalg.svd(block[:fine])[2][:2]
    rest = block[fine:] - (block[fine:] @ first.T) @ first
    second = np.linalg.svd(rest)[2][:2]
    basis = np.concatenate([first, second])
    gains = block @ basis.T
    gains[:fine, 2:] = 0
    return basis, gains


@functools.cache
def operators(n):
    low, high = lift_rows(np.eye(3 * n))
    low2, high2 = lift_rows(low)
    h, q = n // 2, n // 4
    rows = np.concatenate([low[h : 2 * h], high[h : 2 * h], low2[q : 2 * q], high2[q : 2 * q]])
    return rows[:, n : 2 * n], factored(rows[:, :n], n), factored(rows[:, 2 * n :], n)


def halves(w):
    hi = w.astype(ml_dtypes.bfloat16)
    return hi, (w - hi.astype(np.float64)).astype(ml_dtypes.bfloat16)


def three(w, axis):
    hi, lo = halves(w)
    return np.concatenate([hi, hi, lo], axis)


@functools.cache
def constants():
    own_y, (basis_left, gain_left), (basis_right, gain_right) = operators(BY)
    y_low = np.zeros((4, 96, 80))
    for p in range(4):
        y_low[p, :, :64] = own_y
        y_low[p, :, 64 + 2 * p : 66 + 2 * p] = gain_left[:, :2]
        y_low[p, :, 72 + 2 * p : 74 + 2 * p] = gain_right[:, :2]
    y_high = y_low[:, :64]
    y_more = np.zeros((4, 32, 16))
    for p in range(4):
        y_more[p, :, 2 * p : 2 * p + 2] = gain_left[64:, 2:]
        y_more[p, :, 8 + 2 * p : 10 + 2 * p] = gain_right[64:, 2:]
    corner = np.zeros((2, 96, 32))
    for group in range(2):
        for side, gain in enumerate((gain_left, gain_right)):
            for p in range(2):
                at = 16 * p + 8 * side + 2 * group
                corner[group, :, at : at + 2] = gain[:, 2 * p : 2 * p + 2]
    z_one = np.concatenate([own_y, corner[0]], 1)
    z_two = corner[1, 64:]
    coarse_y = own_y[64:]
    edge = np.r_[0:16, 48:64]
    assert abs(np.delete(basis_left, edge, 1)).max() < 1e-12
    assert abs(np.delete(basis_right, edge, 1)).max() < 1e-12
    state_low = np.zeros((64, 256))
    state_high = np.zeros((32, 256))
    for side, basis in enumerate((basis_right, basis_left)):
        for i in range(8):
            columns = slice(32 * i, 32 * i + 32)
            for p in range(2):
                at = 32 * side + 16 * p + 2 * i
                state_low[at : at + 2, columns] = basis[2 * p : 2 * p + 2, edge]
            state_high[16 * side + 2 * i : 16 * side + 2 * i + 2, columns] = basis[:2, edge]

    own_z, (left, gain_l), (right, gain_r) = operators(BZ)
    zs_low = np.concatenate([np.tile(b[p : p + 2].T, (1, 16)) for b in (right, left) for p in (0, 2)], 1)
    zs_high = np.concatenate([np.tile(b[:2].T, (1, 32)) for b in (right, left)], 1)
    coarse_z = np.zeros((2, 384, 128), ml_dtypes.bfloat16)
    for p in range(2):
        coarse_z[p, :, 64 * p : 64 * p + 64] = three(own_z[128:].T, 0)
    coarse_z = coarse_z.reshape(768, 128)

    def spread(rows):
        k = rows.shape[1]
        fine = np.zeros((k, 256))
        fine[:, :64] = rows[:64].T
        fine[:, 128:192] = rows[64:128].T
        coarse = np.zeros((k, 128))
        coarse[:, :64] = rows[128:].T
        return fine, coarse

    main_fine, main_coarse = spread(own_z)
    halo_fine, halo_coarse = spread(np.concatenate([gain_l, gain_r], 1))

    def passes(main, halo):
        hi, lo = halves(main)
        ehi, elo = halves(halo)
        table = np.zeros((4, 512, main.shape[1]), ml_dtypes.bfloat16)
        for i in range(4):
            table[i, :384] = np.concatenate([hi, hi, lo], 0)
            table[i, 384 + 32 * i : 384 + 32 * i + 24] = np.concatenate([ehi, ehi, elo], 0)
        return table

    def places(first):
        p = np.zeros((4, 128, 128))
        for lane in range(128):
            i, s = lane // 2 % 4, first + lane % 2
            p[0, lane, 32 * i + s] = p[0, lane, 32 * i + 16 + s] = 1
            p[1, lane, 32 * i + 8 + s] = 1
            p[2, lane, 32 * i + 4 + s] = p[2, lane, 32 * i + 20 + s] = 1
            p[3, lane, 32 * i + 12 + s] = 1
        return p.reshape(512, 128).astype(ml_dtypes.bfloat16)

    wf, wc = passes(main_fine, halo_fine), passes(main_coarse, halo_coarse)
    send = (
        three(state_low, 1), three(state_high, 1), three(zs_low, 0), three(zs_high, 0), coarse_z, three(coarse_y, 1),
        three(y_low, 2), three(y_high, 2), three(y_more, 2).reshape(128, 48),
    )
    work = (
        three(z_one, 1), three(z_two, 1), three(y_high[2], 1), wf, wc,
        np.concatenate([places(0), places(2)], 0),
    )
    return send, work


def split(v):
    hi = v.astype(BF16)
    return hi, (v - hi.astype(F32)).astype(BF16)


def dot(a, b):
    return jnp.dot(a, b, preferred_element_type=F32)


def lift_loop(count, unroll, load, store):
    k = 2 * count
    s_a, d_a, s_b, d_b, s_c, d_c, s_d = [load(i % k) for i in range(k - 4, k + 3)]
    d_a = d_a + predict_one * (s_a + s_b)
    d_b = d_b + predict_one * (s_b + s_c)
    s_b = s_b + update_one * (d_a + d_b)
    d_c = d_c + predict_one * (s_c + s_d)
    s_c = s_c + update_one * (d_b + d_c)
    d_b = d_b + predict_two * (s_b + s_c)

    def step(j, carry):
        s_now, d_before, s_before, d_done = carry
        for u in range(unroll):
            n = unroll * j + u + 1
            d_now, s_next = load(lax.rem(2 * n + 1, k)), load(lax.rem(2 * n + 2, k))
            d_now = d_now + predict_one * (s_now + s_next)
            s_now = s_now + update_one * (d_before + d_now)
            d_before = d_before + predict_two * (s_before + s_now)
            s_before = s_before + update_two * (d_done + d_before)
            store(n - 1, s_before * scale_factor, d_before * (1.0 / scale_factor))
            s_now, d_before, s_before, d_done = s_next, d_now, s_now, d_before
        return s_now, d_before, s_before, d_done

    lax.fori_loop(0, count // unroll, step, (s_d, d_c, s_c, d_b))


def lift_x(v, x_hi, x_lo, rows):
    def store(n, low, high):
        x_hi[n, rows], x_lo[n, rows] = split(low)
        x_hi[HX + n, rows], x_lo[HX + n, rows] = split(high)

    lift_loop(HX, 16, lambda i: v[i, rows], store)


def find_y_states(x_hi, x_lo, st_low, st_high, coarse_z, y_send):
    more = [[], []]
    for half, table in ((0, st_low), (1, st_high)):
        n = 16
        for g in range(0, 8, 2):
            columns = []
            for u in (g, g + 1):
                parts = []
                for ref in (x_hi, x_lo):
                    for x in range(HX * half + 8 * u, HX * half + 8 * u + 8):
                        parts += [ref[x, 0:16], ref[x, 48:64]]
                columns.append(jnp.concatenate(parts + parts[:16], 0))
            states = dot(table[...], jnp.concatenate(columns, 1))
            for u in (0, 1):
                at = NX * half + n * (g + u)
                for side in (0, 1):
                    first = (n if half else 2 * n) * side
                    lanes = slice(128 * u, 128 * u + 128)
                    y_send[side, at : at + n] = states[first : first + n, lanes]
                    if not half:
                        more[side].append(states[first + n : first + 2 * n, lanes])
    pieces = []
    for part in range(2):
        hi, lo = split(jnp.concatenate(more[0][4 * part : 4 * part + 4] + more[1][4 * part : 4 * part + 4], 0))
        pieces += [hi, lo, hi]
    lifted = dot(jnp.concatenate(pieces, 1), coarse_z[...])
    y_send[0, 2 * NX :] = lifted[:HX]
    y_send[1, 2 * NX :] = lifted[HX:]


def find_z_states(x_hi, x_lo, zs_low, zs_high, coarse_y, z_send, z_raw):
    lane = lax.broadcasted_iota(jnp.int32, (8, 128), 1)

    def states_of(first, n, table, slot):
        hi = x_hi[first : first + n].reshape(n * BY, BZ)
        lo = x_lo[first : first + n].reshape(n * BY, BZ)
        states = dot(jnp.concatenate([hi, lo, hi], 1), table[...]).reshape(n, 8, 8, 128)
        acc = states[0]
        for i in range(1, n):
            acc = jnp.where((slot == i)[None], states[i], acc)
        return acc

    def gathered(pieces, of):
        width = 128 // len(pieces)
        out = None
        for k, piece in enumerate(pieces):
            turn = (width * (k - of)) % 128
            moved = pltpu.roll(piece, turn, 2) if turn else piece
            out = moved if out is None else jnp.where((lane // width == k)[None], moved, out)
        return out.reshape(64, 128)

    low = [states_of(16 * k, 16, zs_low, lane % 32 // 2) for k in range(4)]
    high = [states_of(HX + 32 * k, 32, zs_high, lane % 64 // 2) for k in range(2)]
    columns = []
    for side in range(2):
        z_send[side, 0:64] = gathered(low, 2 * side)
        z_send[side, 64:128] = gathered(high, side)
        second = gathered(low, 2 * side + 1)
        z_raw[side] = second
        hi, lo = split(second)
        columns.append(jnp.concatenate([hi, lo, hi], 0))
    lifted = dot(coarse_y[...], jnp.concatenate(columns, 1))
    z_send[0, 128:160] = lifted[:, :128]
    z_send[1, 128:160] = lifted[:, 128:]


def find_corners(z_send, z_raw, st_low, c_send):
    his, los = [], []
    zeros = jnp.zeros((32, 128), F32)
    for side in range(2):
        for top, low in (
            (z_send[side, 0:16], z_send[side, 48:64]),
            (z_raw[side, 0:16], z_raw[side, 48:64]),
            (z_send[side, 64:80], z_send[side, 112:128]),
            (zeros[:16], zeros[:16]),
        ):
            hi, lo = split(jnp.concatenate([top, low], 0))
            his.append(hi)
            los.append(lo)
    states = dot(st_low[...], jnp.concatenate(his + los + his, 0))
    for y in range(2):
        for z in range(2):
            for p in range(2):
                at = 32 * y + 16 * p + 8 * z
                c_send[2 * y + z, 8 * p : 8 * p + 8] = states[at : at + 8]


STEPS = [(-1, 0), (1, 0), (0, -1), (0, 1), (-1, -1), (-1, 1), (1, -1), (1, 1)]
ORDER = (0, 3, 1, 2)


def exchange_kernel(
    v_hbm, st_low_hbm, st_high_hbm, zs_low_hbm, zs_high_hbm, coarse_z_hbm, coarse_y_hbm,
    y_low_hbm, y_high_hbm, y_more_hbm,
    lhs_low, lhs_high, more, z_recv, c_recv,
    v, x_hi, x_lo, y_send, z_send, z_raw, c_send, y_recv,
    st_low, st_high, zs_low, zs_high, coarse_z, coarse_y, y_low, y_high, y_more, in_sem, send_sem, recv_sem,
):
    my_y, my_z = lax.axis_index("gy"), lax.axis_index("gz")
    n_y, n_z = lax.axis_size("gy"), lax.axis_size("gz")

    def device(step_y, step_z):
        return {
            "gy": lax.rem(my_y + step_y + n_y, n_y),
            "gz": lax.rem(my_z + step_z + n_z, n_z),
        }

    barrier = pltpu.get_barrier_semaphore()
    for step in STEPS:
        pl.semaphore_signal(barrier, inc=1, device_id=device(*step), device_id_type=MESH)

    def load(k, src, dst):
        copy = pltpu.make_async_copy(src, dst, in_sem.at[k])
        copy.start()
        return copy

    def load_rows(c):
        rows = pl.ds(16 * c, 16)
        return load(c, v_hbm.at[:, rows], v.at[:, rows])

    loads = {c: load_rows(c) for c in ORDER[:2]}
    tables = [
        (st_low_hbm, st_low), (st_high_hbm, st_high), (coarse_z_hbm, coarse_z), (zs_low_hbm, zs_low),
        (zs_high_hbm, zs_high), (coarse_y_hbm, coarse_y), (y_low_hbm, y_low), (y_high_hbm, y_high), (y_more_hbm, y_more),
    ]
    for k in (0, 1, 2):
        loads[4 + k] = load(4 + k, *tables[k])
    loads.update({c: load_rows(c) for c in ORDER[2:]})
    for k in range(3, 9):
        loads[4 + k] = load(4 + k, *tables[k])

    def lift(c):
        loads[c].wait()
        lift_x(v, x_hi, x_lo, pl.ds(16 * c, 16))

    def send(k):
        source = (y_send, z_send, c_send)[k // 2 if k < 4 else 2]
        target = (y_recv, z_recv, c_recv)[k // 2 if k < 4 else 2]
        at, to = (k % 2, 1 - k % 2) if k < 4 else (k - 4, 7 - k)
        copy = pltpu.make_async_remote_copy(
            src_ref=source.at[at], dst_ref=target.at[to],
            send_sem=send_sem.at[k], recv_sem=recv_sem.at[k],
            device_id=device(*STEPS[k]), device_id_type=MESH,
        )
        copy.start()
        return copy

    lift(ORDER[0])
    lift(ORDER[1])
    for k in (4, 5, 6):
        loads[k].wait()
    find_y_states(x_hi, x_lo, st_low, st_high, coarse_z, y_send)
    pl.semaphore_wait(barrier, 8)
    y_copies = [send(k) for k in (0, 1)]

    lift(ORDER[2])
    lift(ORDER[3])
    for k in (7, 8, 9):
        loads[k].wait()
    find_z_states(x_hi, x_lo, zs_low, zs_high, coarse_y, z_send, z_raw)
    find_corners(z_send, z_raw, st_low, c_send)
    z_copies = [send(k) for k in range(4, 8)]
    z_copies += [send(k) for k in (2, 3)]

    for k in (10, 11, 12):
        loads[k].wait()
    for copy in y_copies:
        copy.wait()
    lift_more(y_recv, y_more, more)
    for part in range(4):
        lift_y(part, True, x_hi, x_lo, y_recv, y_low, lhs_low)
        lift_y(part, False, x_hi, x_lo, y_recv, y_high, lhs_high)
    for copy in z_copies:
        copy.wait()


def stacked(hi, lo, tiles):
    thi, tlo = split(tiles)
    return jnp.concatenate([hi, thi, lo, tlo, hi, thi], 0)


def lift_z_halos(z_recv, c_recv, z_one, z_two, z_high, places, zh_low, zh_high):
    lane = lax.broadcasted_iota(jnp.int32, (1, 512), 1) % 128
    masks = [jnp.where(lane // 8 == g, 1.0, 0.0).astype(BF16) for g in range(16)]
    first, second, high = [], [], []
    for side in range(2):
        corners = [c_recv[2 * y + side, 8 * p : 8 * p + 8] for p in range(2) for y in range(2)]
        tiles = jnp.concatenate(corners, 0)
        own = z_recv[side]
        first += split(dot(z_one[...], tripled(jnp.concatenate([own[:64], tiles], 0))))
        second += split(own[128:160] + dot(z_two[...], tripled(tiles)))
        high += split(dot(z_high[...], tripled(jnp.concatenate([own[64:128], tiles[:16]], 0))))
    first, second, high = (jnp.concatenate(blocks, 1) for blocks in (first, second, high))
    one = jnp.concatenate([high * m for m in masks], 0)
    zh_high[...] = dot(one, places[:512]).astype(BF16).reshape(16, 64, 128)
    one = jnp.concatenate([first[:64] * m for m in masks], 0)
    zh_low[:, :64] = dot(one, places[:512]).astype(BF16).reshape(16, 64, 128)
    both = [jnp.concatenate([first[64:] * m, second * m], 1) for m in masks]
    both = dot(jnp.concatenate(both, 0), places[...])
    zh_low[:, 64:] = both.astype(BF16).reshape(16, 32, 128)


def tripled(v):
    hi, lo = split(v)
    return jnp.concatenate([hi, lo, hi], 0)


def lift_more(y_recv, y_more, more):
    for t in range(0, 8, 2):
        columns = []
        for u in (t, t + 1):
            at = 2 * NX + 8 * u
            columns.append(tripled(jnp.concatenate([y_recv[0, at : at + 8], y_recv[1, at : at + 8]], 0)))
        lifted = dot(y_more[...], jnp.concatenate(columns, 1))
        for u in (0, 1):
            for i in range(4):
                value = lifted[32 * i : 32 * i + 32, 128 * u : 128 * u + 128]
                x = 4 * (t + u) + i
                more[x] = value
                more[HX // 2 + x] = pltpu.roll(value, 64, 1)


def lift_y(part, low, x_hi, x_lo, y_recv, table, lhs):
    first = 0 if low else HX
    for i in range(4):
        for q in range(0, 4, 2):
            columns = []
            for u in (q, q + 1):
                x = first + 16 * part + 4 * u + i
                at = 8 * (x // 4)
                tiles = jnp.concatenate([y_recv[0, at : at + 8], y_recv[1, at : at + 8]], 0)
                columns.append(stacked(x_hi[x], x_lo[x], tiles))
            hi, lo = split(dot(table[i], jnp.concatenate(columns, 1)))
            for u in (0, 1):
                lhs[0, part, i, q + u] = hi[:, 128 * u : 128 * u + 128]
                lhs[1, part, i, q + u] = lo[:, 128 * u : 128 * u + 128]


def lift_z(part, i, zh, lhs, table, start, rows):
    hi = lhs[0, part, i, :, start : start + rows].reshape(4 * rows, 128)
    lo = lhs[1, part, i, :, start : start + rows].reshape(4 * rows, 128)
    zh = zh[4 * part : 4 * part + 4, start : start + rows].reshape(4 * rows, 128)
    return dot(jnp.concatenate([hi, lo, hi, zh], 1), table[i])


def low_part(part, lhs, more, zh_low, wf, wc, fine, level):
    for i in range(4):
        one = lift_z(part, i, zh_low, lhs, wf, 0, 64)
        two = lift_z(part, i, zh_low, lhs, wc, 64, 32)
        for q in range(4):
            x = 16 * part + 4 * q + i
            fine[0, x] = one[64 * q : 64 * q + 32, 128:192]
            fine[1, x] = one[64 * q + 32 : 64 * q + 64, :64]
            fine[2, x] = one[64 * q + 32 : 64 * q + 64, 128:192]
            level[x] = two[32 * q : 32 * q + 32] + more[x]


def high_part(part, lhs, zh_high, wf, fine):
    for i in range(4):
        one = lift_z(part, i, zh_high, lhs, wf, 0, 64)
        for q in range(4):
            x = 16 * part + 4 * q + i
            fine[3, x] = one[64 * q : 64 * q + 32, :64]
            fine[4, x] = one[64 * q : 64 * q + 32, 128:192]
            fine[5, x] = one[64 * q + 32 : 64 * q + 64, :64]
            fine[6, x] = one[64 * q + 32 : 64 * q + 64, 128:192]


def lift_level(level, coarse):
    def store(n, low, high):
        for bx, value in enumerate((low, high)):
            for by in range(2):
                for bz in range(2):
                    coarse[4 * bx + 2 * by + bz, n] = value[
                        16 * by : 16 * by + 16, 32 * bz : 32 * bz + 32
                    ]

    lift_loop(HX // 2, 16, lambda i: level[i], store)


def finish_kernel(
    lhs_low, lhs_high, more, z_recv, c_recv, z_one, z_two, z_high, wf, wc, places,
    fine_hbm, coarse_hbm,
    fine, coarse, level, zh_low, zh_high, sem,
):
    copies = []

    def write(bands, part):
        at = pl.ds(16 * part, 16)
        src, dst = fine.at[pl.ds(*bands), at], fine_hbm.at[pl.ds(*bands), at]
        copies.append(pltpu.make_async_copy(src, dst, sem.at[part + (4 if bands == HIGH_BANDS else 0)]))
        copies[-1].start()

    lift_z_halos(z_recv, c_recv, z_one, z_two, z_high, places, zh_low, zh_high)
    for part in range(4):
        low_part(part, lhs_low, more, zh_low, wf, wc, fine, level)
        write(LOW_BANDS, part)
    lift_level(level, coarse)
    copies.append(pltpu.make_async_copy(coarse, coarse_hbm, sem.at[8]))
    copies[-1].start()
    for part in range(4):
        high_part(part, lhs_high, zh_high, wf, fine)
        write(HIGH_BANDS, part)
    for copy in copies:
        copy.wait()


LOW_BANDS, HIGH_BANDS = (0, 3), (3, 4)


def body(velocity):
    send, work = constants()
    vmem = pl.BlockSpec(memory_space=pltpu.VMEM)
    hbm = pl.BlockSpec(memory_space=pltpu.HBM)
    shape = jax.ShapeDtypeStruct
    y_shape, z_shape, c_shape = (2, Y_ROWS, BZ), (2, Z_ROWS, 128), (4, 16, 128)
    halos = pl.pallas_call(
        exchange_kernel,
        out_shape=(
            shape((2, 4, 4, 4, 96, 128), BF16), shape((2, 4, 4, 4, 64, 128), BF16),
            shape((HX, 32, 128), F32), shape(z_shape, F32), shape(c_shape, F32),
        ),
        in_specs=[hbm] * 10,
        out_specs=(vmem,) * 5,
        scratch_shapes=[
            pltpu.VMEM((NX, BY, BZ), F32),
            pltpu.VMEM((NX, BY, BZ), BF16),
            pltpu.VMEM((NX, BY, BZ), BF16),
            pltpu.VMEM(y_shape, F32),
            pltpu.VMEM(z_shape, F32),
            pltpu.VMEM((2, BY, 128), F32),
            pltpu.VMEM(c_shape, F32),
            pltpu.VMEM(y_shape, F32),
            *[pltpu.VMEM(a.shape, BF16) for a in send],
            pltpu.SemaphoreType.DMA((13,)),
            pltpu.SemaphoreType.DMA((8,)),
            pltpu.SemaphoreType.DMA((8,)),
        ],
        compiler_params=pltpu.CompilerParams(
            collective_id=0, has_side_effects=True, vmem_limit_bytes=32 * 2**20
        ),
        name="exchange",
    )(*[pltpu.with_memory_space_constraint(jnp.asarray(a), pltpu.HBM) for a in (velocity, *send)])
    fine_shape, coarse_shape = (7, HX, BY // 2, BZ // 2), (8, HX // 2, BY // 4, BZ // 4)
    return pl.pallas_call(
        finish_kernel,
        out_shape=(shape(fine_shape, F32), shape(coarse_shape, F32)),
        in_specs=[vmem] * 11,
        out_specs=(hbm, hbm),
        scratch_shapes=[
            pltpu.VMEM(fine_shape, F32),
            pltpu.VMEM(coarse_shape, F32),
            pltpu.VMEM((HX, 32, 128), F32),
            pltpu.VMEM((16, 96, 128), BF16),
            pltpu.VMEM((16, 64, 128), BF16),
            pltpu.SemaphoreType.DMA((9,)),
        ],
        compiler_params=pltpu.CompilerParams(vmem_limit_bytes=28 * 2**20),
        name="finish",
    )(*halos, *[jnp.asarray(a) for a in work])


def solution(mesh):
    return jax.shard_map(
        body,
        mesh=mesh,
        in_specs=(P(None, "gy", "gz"),),
        out_specs=(P(None, None, "gy", "gz"), P(None, None, "gy", "gz")),
        check_vma=False,
    )
```

```python
import functools

import jax
import jax.numpy as jnp
import ml_dtypes
import numpy as np
from jax import lax
from jax.experimental import pallas as pl
from jax.experimental.pallas import tpu as pltpu
from jax.sharding import PartitionSpec as P

predict_one = -1.586134342
update_one = -0.05298011854
predict_two = 0.8829110762
update_two = 0.4435068522
scale_factor = 1.149604398

MESH = pl.DeviceIdType.MESH
F32 = jnp.float32
BF16 = jnp.bfloat16
NX, HX = 128, 64
BY, BZ = 64, 128
Y_ROWS = 2 * NX + HX
Z_ROWS = 2 * BY + BY // 2


def lift_rows(v):
    s, d = v[0::2], v[1::2]
    d = d + predict_one * (s + np.roll(s, -1, 0))
    s = s + update_one * (np.roll(d, 1, 0) + d)
    d = d + predict_two * (s + np.roll(s, -1, 0))
    s = s + update_two * (np.roll(d, 1, 0) + d)
    return s * scale_factor, d / scale_factor


def factored(block, fine):
    first = np.linalg.svd(block[:fine])[2][:2]
    rest = block[fine:] - (block[fine:] @ first.T) @ first
    second = np.linalg.svd(rest)[2][:2]
    basis = np.concatenate([first, second])
    gains = block @ basis.T
    gains[:fine, 2:] = 0
    return basis, gains


@functools.cache
def operators(n):
    low, high = lift_rows(np.eye(3 * n))
    low2, high2 = lift_rows(low)
    h, q = n // 2, n // 4
    rows = np.concatenate([low[h : 2 * h], high[h : 2 * h], low2[q : 2 * q], high2[q : 2 * q]])
    return rows[:, n : 2 * n], factored(rows[:, :n], n), factored(rows[:, 2 * n :], n)


def halves(w):
    hi = w.astype(ml_dtypes.bfloat16)
    return hi, (w - hi.astype(np.float64)).astype(ml_dtypes.bfloat16)


def three(w, axis):
    hi, lo = halves(w)
    return np.concatenate([hi, hi, lo], axis)


@functools.cache
def constants():
    own_y, (basis_left, gain_left), (basis_right, gain_right) = operators(BY)
    y_low = np.zeros((4, 96, 80))
    for p in range(4):
        y_low[p, :, :64] = own_y
        y_low[p, :, 64 + 2 * p : 66 + 2 * p] = gain_left[:, :2]
        y_low[p, :, 72 + 2 * p : 74 + 2 * p] = gain_right[:, :2]
    y_high = y_low[:, :64]
    y_more = np.zeros((4, 32, 16))
    for p in range(4):
        y_more[p, :, 2 * p : 2 * p + 2] = gain_left[64:, 2:]
        y_more[p, :, 8 + 2 * p : 10 + 2 * p] = gain_right[64:, 2:]
    corner = np.zeros((2, 96, 32))
    for group in range(2):
        for side, gain in enumerate((gain_left, gain_right)):
            for p in range(2):
                at = 16 * p + 8 * side + 2 * group
                corner[group, :, at : at + 2] = gain[:, 2 * p : 2 * p + 2]
    z_one = np.concatenate([own_y, corner[0]], 1)
    z_two = corner[1, 64:]
    coarse_y = own_y[64:]
    edge = np.r_[0:16, 48:64]
    assert abs(np.delete(basis_left, edge, 1)).max() < 1e-12
    assert abs(np.delete(basis_right, edge, 1)).max() < 1e-12
    state_low = np.zeros((64, 256))
    state_high = np.zeros((32, 256))
    for side, basis in enumerate((basis_right, basis_left)):
        for i in range(8):
            columns = slice(32 * i, 32 * i + 32)
            for p in range(2):
                at = 32 * side + 16 * p + 2 * i
                state_low[at : at + 2, columns] = basis[2 * p : 2 * p + 2, edge]
            state_high[16 * side + 2 * i : 16 * side + 2 * i + 2, columns] = basis[:2, edge]

    own_z, (left, gain_l), (right, gain_r) = operators(BZ)
    zs_low = np.concatenate([np.tile(b[p : p + 2].T, (1, 16)) for b in (right, left) for p in (0, 2)], 1)
    zs_high = np.concatenate([np.tile(b[:2].T, (1, 32)) for b in (right, left)], 1)
    coarse_z = np.zeros((2, 384, 128), ml_dtypes.bfloat16)
    for p in range(2):
        coarse_z[p, :, 64 * p : 64 * p + 64] = three(own_z[128:].T, 0)
    coarse_z = coarse_z.reshape(768, 128)

    def spread(rows):
        k = rows.shape[1]
        fine = np.zeros((k, 256))
        fine[:, :64] = rows[:64].T
        fine[:, 128:192] = rows[64:128].T
        coarse = np.zeros((k, 128))
        coarse[:, :64] = rows[128:].T
        return fine, coarse

    main_fine, main_coarse = spread(own_z)
    halo_fine, halo_coarse = spread(np.concatenate([gain_l, gain_r], 1))

    def passes(main, halo):
        hi, lo = halves(main)
        ehi, elo = halves(halo)
        table = np.zeros((4, 512, main.shape[1]), ml_dtypes.bfloat16)
        for i in range(4):
            table[i, :384] = np.concatenate([hi, hi, lo], 0)
            table[i, 384 + 32 * i : 384 + 32 * i + 24] = np.concatenate([ehi, ehi, elo], 0)
        return table

    def places(first):
        p = np.zeros((4, 128, 128))
        for lane in range(128):
            i, s = lane // 2 % 4, first + lane % 2
            p[0, lane, 32 * i + s] = p[0, lane, 32 * i + 16 + s] = 1
            p[1, lane, 32 * i + 8 + s] = 1
            p[2, lane, 32 * i + 4 + s] = p[2, lane, 32 * i + 20 + s] = 1
            p[3, lane, 32 * i + 12 + s] = 1
        return p.reshape(512, 128).astype(ml_dtypes.bfloat16)

    wf, wc = passes(main_fine, halo_fine), passes(main_coarse, halo_coarse)
    send = (
        three(state_low, 1), three(state_high, 1), three(zs_low, 0), three(zs_high, 0), coarse_z, three(coarse_y, 1),
        three(y_low, 2), three(y_high, 2), three(y_more, 2).reshape(128, 48),
    )
    work = (
        three(z_one, 1), three(z_two, 1), three(y_high[2], 1), wf, wc,
        np.concatenate([places(0), places(2)], 0),
    )
    return send, work


def split(v):
    hi = v.astype(BF16)
    return hi, (v - hi.astype(F32)).astype(BF16)


def dot(a, b):
    return jnp.dot(a, b, preferred_element_type=F32)


def lift_loop(count, unroll, load, store):
    k = 2 * count
    s_a, d_a, s_b, d_b, s_c, d_c, s_d = [load(i % k) for i in range(k - 4, k + 3)]
    d_a = d_a + predict_one * (s_a + s_b)
    d_b = d_b + predict_one * (s_b + s_c)
    s_b = s_b + update_one * (d_a + d_b)
    d_c = d_c + predict_one * (s_c + s_d)
    s_c = s_c + update_one * (d_b + d_c)
    d_b = d_b + predict_two * (s_b + s_c)

    def step(j, carry):
        s_now, d_before, s_before, d_done = carry
        for u in range(unroll):
            n = unroll * j + u + 1
            d_now, s_next = load(lax.rem(2 * n + 1, k)), load(lax.rem(2 * n + 2, k))
            d_now = d_now + predict_one * (s_now + s_next)
            s_now = s_now + update_one * (d_before + d_now)
            d_before = d_before + predict_two * (s_before + s_now)
            s_before = s_before + update_two * (d_done + d_before)
            store(n - 1, s_before * scale_factor, d_before * (1.0 / scale_factor))
            s_now, d_before, s_before, d_done = s_next, d_now, s_now, d_before
        return s_now, d_before, s_before, d_done

    lax.fori_loop(0, count // unroll, step, (s_d, d_c, s_c, d_b))


def lift_x(v, x_hi, x_lo, rows):
    def store(n, low, high):
        x_hi[n, rows], x_lo[n, rows] = split(low)
        x_hi[HX + n, rows], x_lo[HX + n, rows] = split(high)

    lift_loop(HX, 16, lambda i: v[i, rows], store)


def find_y_states(x_hi, x_lo, st_low, st_high, coarse_z, y_send):
    more = [[], []]
    for half, table in ((0, st_low), (1, st_high)):
        n = 16
        for g in range(0, 8, 2):
            columns = []
            for u in (g, g + 1):
                parts = []
                for ref in (x_hi, x_lo):
                    for x in range(HX * half + 8 * u, HX * half + 8 * u + 8):
                        parts += [ref[x, 0:16], ref[x, 48:64]]
                columns.append(jnp.concatenate(parts + parts[:16], 0))
            states = dot(table[...], jnp.concatenate(columns, 1))
            for u in (0, 1):
                at = NX * half + n * (g + u)
                for side in (0, 1):
                    first = (n if half else 2 * n) * side
                    lanes = slice(128 * u, 128 * u + 128)
                    y_send[side, at : at + n] = states[first : first + n, lanes]
                    if not half:
                        more[side].append(states[first + n : first + 2 * n, lanes])
    pieces = []
    for part in range(2):
        hi, lo = split(jnp.concatenate(more[0][4 * part : 4 * part + 4] + more[1][4 * part : 4 * part + 4], 0))
        pieces += [hi, lo, hi]
    lifted = dot(jnp.concatenate(pieces, 1), coarse_z[...])
    y_send[0, 2 * NX :] = lifted[:HX]
    y_send[1, 2 * NX :] = lifted[HX:]


def find_z_states(x_hi, x_lo, zs_low, zs_high, coarse_y, z_send, z_raw):
    lane = lax.broadcasted_iota(jnp.int32, (8, 128), 1)

    def states_of(first, n, table, slot):
        hi = x_hi[first : first + n].reshape(n * BY, BZ)
        lo = x_lo[first : first + n].reshape(n * BY, BZ)
        states = dot(jnp.concatenate([hi, lo, hi], 1), table[...]).reshape(n, 8, 8, 128)
        acc = states[0]
        for i in range(1, n):
            acc = jnp.where((slot == i)[None], states[i], acc)
        return acc

    def gathered(pieces, of):
        width = 128 // len(pieces)
        out = None
        for k, piece in enumerate(pieces):
            turn = (width * (k - of)) % 128
            moved = pltpu.roll(piece, turn, 2) if turn else piece
            out = moved if out is None else jnp.where((lane // width == k)[None], moved, out)
        return out.reshape(64, 128)

    low = [states_of(16 * k, 16, zs_low, lane % 32 // 2) for k in range(4)]
    high = [states_of(HX + 32 * k, 32, zs_high, lane % 64 // 2) for k in range(2)]
    columns = []
    for side in range(2):
        z_send[side, 0:64] = gathered(low, 2 * side)
        z_send[side, 64:128] = gathered(high, side)
        second = gathered(low, 2 * side + 1)
        z_raw[side] = second
        hi, lo = split(second)
        columns.append(jnp.concatenate([hi, lo, hi], 0))
    lifted = dot(coarse_y[...], jnp.concatenate(columns, 1))
    z_send[0, 128:160] = lifted[:, :128]
    z_send[1, 128:160] = lifted[:, 128:]


def find_corners(z_send, z_raw, st_low, c_send):
    his, los = [], []
    zeros = jnp.zeros((32, 128), F32)
    for side in range(2):
        for top, low in (
            (z_send[side, 0:16], z_send[side, 48:64]),
            (z_raw[side, 0:16], z_raw[side, 48:64]),
            (z_send[side, 64:80], z_send[side, 112:128]),
            (zeros[:16], zeros[:16]),
        ):
            hi, lo = split(jnp.concatenate([top, low], 0))
            his.append(hi)
            los.append(lo)
    states = dot(st_low[...], jnp.concatenate(his + los + his, 0))
    for y in range(2):
        for z in range(2):
            for p in range(2):
                at = 32 * y + 16 * p + 8 * z
                c_send[2 * y + z, 8 * p : 8 * p + 8] = states[at : at + 8]


STEPS = [(-1, 0), (1, 0), (0, -1), (0, 1), (-1, -1), (-1, 1), (1, -1), (1, 1)]
ORDER = (0, 3, 1, 2)


def exchange_kernel(
    v_hbm, st_low_hbm, st_high_hbm, zs_low_hbm, zs_high_hbm, coarse_z_hbm, coarse_y_hbm,
    y_low_hbm, y_high_hbm, y_more_hbm,
    lhs_low, lhs_high, more, z_recv, c_recv,
    v, x_hi, x_lo, y_send, z_send, z_raw, c_send, y_recv,
    st_low, st_high, zs_low, zs_high, coarse_z, coarse_y, y_low, y_high, y_more, in_sem, send_sem, recv_sem,
):
    my_y, my_z = lax.axis_index("gy"), lax.axis_index("gz")
    n_y, n_z = lax.axis_size("gy"), lax.axis_size("gz")

    def device(step_y, step_z):
        return {
            "gy": lax.rem(my_y + step_y + n_y, n_y),
            "gz": lax.rem(my_z + step_z + n_z, n_z),
        }

    barrier = pltpu.get_barrier_semaphore()
    for step in STEPS:
        pl.semaphore_signal(barrier, inc=1, device_id=device(*step), device_id_type=MESH)

    def load(k, src, dst):
        copy = pltpu.make_async_copy(src, dst, in_sem.at[k])
        copy.start()
        return copy

    def load_rows(c):
        rows = pl.ds(16 * c, 16)
        return load(c, v_hbm.at[:, rows], v.at[:, rows])

    loads = {c: load_rows(c) for c in ORDER[:2]}
    tables = [
        (st_low_hbm, st_low), (st_high_hbm, st_high), (coarse_z_hbm, coarse_z), (zs_low_hbm, zs_low),
        (zs_high_hbm, zs_high), (coarse_y_hbm, coarse_y), (y_low_hbm, y_low), (y_high_hbm, y_high), (y_more_hbm, y_more),
    ]
    for k in (0, 1, 2):
        loads[4 + k] = load(4 + k, *tables[k])
    loads.update({c: load_rows(c) for c in ORDER[2:]})
    for k in range(3, 9):
        loads[4 + k] = load(4 + k, *tables[k])

    def lift(c):
        loads[c].wait()
        lift_x(v, x_hi, x_lo, pl.ds(16 * c, 16))

    def send(k):
        source = (y_send, z_send, c_send)[k // 2 if k < 4 else 2]
        target = (y_recv, z_recv, c_recv)[k // 2 if k < 4 else 2]
        at, to = (k % 2, 1 - k % 2) if k < 4 else (k - 4, 7 - k)
        copy = pltpu.make_async_remote_copy(
            src_ref=source.at[at], dst_ref=target.at[to],
            send_sem=send_sem.at[k], recv_sem=recv_sem.at[k],
            device_id=device(*STEPS[k]), device_id_type=MESH,
        )
        copy.start()
        return copy

    lift(ORDER[0])
    lift(ORDER[1])
    for k in (4, 5, 6):
        loads[k].wait()
    find_y_states(x_hi, x_lo, st_low, st_high, coarse_z, y_send)
    pl.semaphore_wait(barrier, 8)
    y_copies = [send(k) for k in (0, 1)]

    lift(ORDER[2])
    lift(ORDER[3])
    for k in (7, 8, 9):
        loads[k].wait()
    find_z_states(x_hi, x_lo, zs_low, zs_high, coarse_y, z_send, z_raw)
    find_corners(z_send, z_raw, st_low, c_send)
    z_copies = [send(k) for k in range(4, 8)]
    z_copies += [send(k) for k in (2, 3)]

    for k in (10, 11, 12):
        loads[k].wait()
    for copy in y_copies:
        copy.wait()
    lift_more(y_recv, y_more, more)
    for part in range(4):
        lift_y(part, True, x_hi, x_lo, y_recv, y_low, lhs_low)
        lift_y(part, False, x_hi, x_lo, y_recv, y_high, lhs_high)
    for copy in z_copies:
        copy.wait()


def stacked(hi, lo, tiles):
    thi, tlo = split(tiles)
    return jnp.concatenate([hi, thi, lo, tlo, hi, thi], 0)


def lift_z_halos(z_recv, c_recv, z_one, z_two, z_high, places, zh_low, zh_high):
    lane = lax.broadcasted_iota(jnp.int32, (1, 512), 1) % 128
    masks = [jnp.where(lane // 8 == g, 1.0, 0.0).astype(BF16) for g in range(16)]
    first, second, high = [], [], []
    for side in range(2):
        corners = [c_recv[2 * y + side, 8 * p : 8 * p + 8] for p in range(2) for y in range(2)]
        tiles = jnp.concatenate(corners, 0)
        own = z_recv[side]
        first += split(dot(z_one[...], tripled(jnp.concatenate([own[:64], tiles], 0))))
        second += split(own[128:160] + dot(z_two[...], tripled(tiles)))
        high += split(dot(z_high[...], tripled(jnp.concatenate([own[64:128], tiles[:16]], 0))))
    first, second, high = (jnp.concatenate(blocks, 1) for blocks in (first, second, high))
    one = jnp.concatenate([high * m for m in masks], 0)
    zh_high[...] = dot(one, places[:512]).astype(BF16).reshape(16, 64, 128)
    one = jnp.concatenate([first[:64] * m for m in masks], 0)
    zh_low[:, :64] = dot(one, places[:512]).astype(BF16).reshape(16, 64, 128)
    both = [jnp.concatenate([first[64:] * m, second * m], 1) for m in masks]
    both = dot(jnp.concatenate(both, 0), places[...])
    zh_low[:, 64:] = both.astype(BF16).reshape(16, 32, 128)


def tripled(v):
    hi, lo = split(v)
    return jnp.concatenate([hi, lo, hi], 0)


def lift_more(y_recv, y_more, more):
    for t in range(0, 8, 2):
        columns = []
        for u in (t, t + 1):
            at = 2 * NX + 8 * u
            columns.append(tripled(jnp.concatenate([y_recv[0, at : at + 8], y_recv[1, at : at + 8]], 0)))
        lifted = dot(y_more[...], jnp.concatenate(columns, 1))
        for u in (0, 1):
            for i in range(4):
                value = lifted[32 * i : 32 * i + 32, 128 * u : 128 * u + 128]
                x = 4 * (t + u) + i
                more[x] = value
                more[HX // 2 + x] = pltpu.roll(value, 64, 1)


def lift_y(part, low, x_hi, x_lo, y_recv, table, lhs):
    first = 0 if low else HX
    for i in range(4):
        for q in range(0, 4, 2):
            columns = []
            for u in (q, q + 1):
                x = first + 16 * part + 4 * u + i
                at = 8 * (x // 4)
                tiles = jnp.concatenate([y_recv[0, at : at + 8], y_recv[1, at : at + 8]], 0)
                columns.append(stacked(x_hi[x], x_lo[x], tiles))
            hi, lo = split(dot(table[i], jnp.concatenate(columns, 1)))
            for u in (0, 1):
                lhs[0, part, i, q + u] = hi[:, 128 * u : 128 * u + 128]
                lhs[1, part, i, q + u] = lo[:, 128 * u : 128 * u + 128]


def lift_z(part, i, zh, lhs, table, start, rows):
    hi = lhs[0, part, i, :, start : start + rows].reshape(4 * rows, 128)
    lo = lhs[1, part, i, :, start : start + rows].reshape(4 * rows, 128)
    zh = zh[4 * part : 4 * part + 4, start : start + rows].reshape(4 * rows, 128)
    return dot(jnp.concatenate([hi, lo, hi, zh], 1), table[i])


def low_part(part, lhs, more, zh_low, wf, wc, fine, level):
    for i in range(4):
        one = lift_z(part, i, zh_low, lhs, wf, 0, 64)
        two = lift_z(part, i, zh_low, lhs, wc, 64, 32)
        for q in range(4):
            x = 16 * part + 4 * q + i
            fine[0, x] = one[64 * q : 64 * q + 32, 128:192]
            fine[1, x] = one[64 * q + 32 : 64 * q + 64, :64]
            fine[2, x] = one[64 * q + 32 : 64 * q + 64, 128:192]
            level[x] = two[32 * q : 32 * q + 32] + more[x]


def high_part(part, lhs, zh_high, wf, fine):
    for i in range(4):
        one = lift_z(part, i, zh_high, lhs, wf, 0, 64)
        for q in range(4):
            x = 16 * part + 4 * q + i
            fine[3, x] = one[64 * q : 64 * q + 32, :64]
            fine[4, x] = one[64 * q : 64 * q + 32, 128:192]
            fine[5, x] = one[64 * q + 32 : 64 * q + 64, :64]
            fine[6, x] = one[64 * q + 32 : 64 * q + 64, 128:192]


def lift_level(level, coarse):
    def store(n, low, high):
        for bx, value in enumerate((low, high)):
            for by in range(2):
                for bz in range(2):
                    coarse[4 * bx + 2 * by + bz, n] = value[
                        16 * by : 16 * by + 16, 32 * bz : 32 * bz + 32
                    ]

    lift_loop(HX // 2, 16, lambda i: level[i], store)


def finish_kernel(
    lhs_low, lhs_high, more, z_recv, c_recv, z_one, z_two, z_high, wf, wc, places,
    fine_hbm, coarse_hbm,
    fine, coarse, level, zh_low, zh_high, sem,
):
    copies = []

    def write(bands, part):
        at = pl.ds(16 * part, 16)
        src, dst = fine.at[pl.ds(*bands), at], fine_hbm.at[pl.ds(*bands), at]
        copies.append(pltpu.make_async_copy(src, dst, sem.at[part + (4 if bands == HIGH_BANDS else 0)]))
        copies[-1].start()

    lift_z_halos(z_recv, c_recv, z_one, z_two, z_high, places, zh_low, zh_high)

    def low(part):
        low_part(part, lhs_low, more, zh_low, wf, wc, fine, level)
        write(LOW_BANDS, part)

    def high(part):
        high_part(part, lhs_high, zh_high, wf, fine)
        write(HIGH_BANDS, part)

    def last():
        lift_level(level, coarse)
        copies.append(pltpu.make_async_copy(coarse, coarse_hbm, sem.at[8]))
        copies[-1].start()

    high(0)
    high(1)
    low(0)
    low(1)
    low(2)
    low(3)
    last()
    high(2)
    high(3)
    for copy in copies:
        copy.wait()


LOW_BANDS, HIGH_BANDS = (0, 3), (3, 4)


def body(velocity):
    send, work = constants()
    vmem = pl.BlockSpec(memory_space=pltpu.VMEM)
    hbm = pl.BlockSpec(memory_space=pltpu.HBM)
    shape = jax.ShapeDtypeStruct
    y_shape, z_shape, c_shape = (2, Y_ROWS, BZ), (2, Z_ROWS, 128), (4, 16, 128)
    halos = pl.pallas_call(
        exchange_kernel,
        out_shape=(
            shape((2, 4, 4, 4, 96, 128), BF16), shape((2, 4, 4, 4, 64, 128), BF16),
            shape((HX, 32, 128), F32), shape(z_shape, F32), shape(c_shape, F32),
        ),
        in_specs=[hbm] * 10,
        out_specs=(vmem,) * 5,
        scratch_shapes=[
            pltpu.VMEM((NX, BY, BZ), F32),
            pltpu.VMEM((NX, BY, BZ), BF16),
            pltpu.VMEM((NX, BY, BZ), BF16),
            pltpu.VMEM(y_shape, F32),
            pltpu.VMEM(z_shape, F32),
            pltpu.VMEM((2, BY, 128), F32),
            pltpu.VMEM(c_shape, F32),
            pltpu.VMEM(y_shape, F32),
            *[pltpu.VMEM(a.shape, BF16) for a in send],
            pltpu.SemaphoreType.DMA((13,)),
            pltpu.SemaphoreType.DMA((8,)),
            pltpu.SemaphoreType.DMA((8,)),
        ],
        compiler_params=pltpu.CompilerParams(
            collective_id=0, has_side_effects=True, vmem_limit_bytes=32 * 2**20
        ),
        name="exchange",
    )(*[pltpu.with_memory_space_constraint(jnp.asarray(a), pltpu.HBM) for a in (velocity, *send)])
    fine_shape, coarse_shape = (7, HX, BY // 2, BZ // 2), (8, HX // 2, BY // 4, BZ // 4)
    return pl.pallas_call(
        finish_kernel,
        out_shape=(shape(fine_shape, F32), shape(coarse_shape, F32)),
        in_specs=[vmem] * 11,
        out_specs=(hbm, hbm),
        scratch_shapes=[
            pltpu.VMEM(fine_shape, F32),
            pltpu.VMEM(coarse_shape, F32),
            pltpu.VMEM((HX, 32, 128), F32),
            pltpu.VMEM((16, 96, 128), BF16),
            pltpu.VMEM((16, 64, 128), BF16),
            pltpu.SemaphoreType.DMA((9,)),
        ],
        compiler_params=pltpu.CompilerParams(vmem_limit_bytes=28 * 2**20),
        name="finish",
    )(*halos, *[jnp.asarray(a) for a in work])


def solution(mesh):
    return jax.shard_map(
        body,
        mesh=mesh,
        in_specs=(P(None, "gy", "gz"),),
        out_specs=(P(None, None, "gy", "gz"), P(None, None, "gy", "gz")),
        check_vma=False,
    )
```

```python
import functools

import jax
import jax.numpy as jnp
import ml_dtypes
import numpy as np
from jax import lax
from jax.experimental import pallas as pl
from jax.experimental.pallas import tpu as pltpu
from jax.sharding import PartitionSpec as P

predict_one = -1.586134342
update_one = -0.05298011854
predict_two = 0.8829110762
update_two = 0.4435068522
scale_factor = 1.149604398

MESH = pl.DeviceIdType.MESH
F32 = jnp.float32
BF16 = jnp.bfloat16
NX, HX = 128, 64
BY, BZ = 64, 128
Y_ROWS = 2 * NX + HX
Z_ROWS = 2 * BY + BY // 2


def lift_rows(v):
    s, d = v[0::2], v[1::2]
    d = d + predict_one * (s + np.roll(s, -1, 0))
    s = s + update_one * (np.roll(d, 1, 0) + d)
    d = d + predict_two * (s + np.roll(s, -1, 0))
    s = s + update_two * (np.roll(d, 1, 0) + d)
    return s * scale_factor, d / scale_factor


def factored(block, fine):
    first = np.linalg.svd(block[:fine])[2][:2]
    rest = block[fine:] - (block[fine:] @ first.T) @ first
    second = np.linalg.svd(rest)[2][:2]
    basis = np.concatenate([first, second])
    gains = block @ basis.T
    gains[:fine, 2:] = 0
    return basis, gains


@functools.cache
def operators(n):
    low, high = lift_rows(np.eye(3 * n))
    low2, high2 = lift_rows(low)
    h, q = n // 2, n // 4
    rows = np.concatenate([low[h : 2 * h], high[h : 2 * h], low2[q : 2 * q], high2[q : 2 * q]])
    return rows[:, n : 2 * n], factored(rows[:, :n], n), factored(rows[:, 2 * n :], n)


def halves(w):
    hi = w.astype(ml_dtypes.bfloat16)
    return hi, (w - hi.astype(np.float64)).astype(ml_dtypes.bfloat16)


def three(w, axis):
    hi, lo = halves(w)
    return np.concatenate([hi, hi, lo], axis)


@functools.cache
def constants():
    own_y, (basis_left, gain_left), (basis_right, gain_right) = operators(BY)
    y_low = np.zeros((4, 96, 80))
    for p in range(4):
        y_low[p, :, :64] = own_y
        y_low[p, :, 64 + 2 * p : 66 + 2 * p] = gain_left[:, :2]
        y_low[p, :, 72 + 2 * p : 74 + 2 * p] = gain_right[:, :2]
    y_high = y_low[:, :64]
    y_more = np.zeros((4, 32, 16))
    for p in range(4):
        y_more[p, :, 2 * p : 2 * p + 2] = gain_left[64:, 2:]
        y_more[p, :, 8 + 2 * p : 10 + 2 * p] = gain_right[64:, 2:]
    corner = np.zeros((2, 96, 32))
    for group in range(2):
        for side, gain in enumerate((gain_left, gain_right)):
            for p in range(2):
                at = 16 * p + 8 * side + 2 * group
                corner[group, :, at : at + 2] = gain[:, 2 * p : 2 * p + 2]
    z_one = np.concatenate([own_y, corner[0]], 1)
    z_two = corner[1, 64:]
    coarse_y = own_y[64:]
    edge = np.r_[0:16, 48:64]
    assert abs(np.delete(basis_left, edge, 1)).max() < 1e-12
    assert abs(np.delete(basis_right, edge, 1)).max() < 1e-12
    state_low = np.zeros((64, 256))
    state_high = np.zeros((32, 256))
    for side, basis in enumerate((basis_right, basis_left)):
        for i in range(8):
            columns = slice(32 * i, 32 * i + 32)
            for p in range(2):
                at = 32 * side + 16 * p + 2 * i
                state_low[at : at + 2, columns] = basis[2 * p : 2 * p + 2, edge]
            state_high[16 * side + 2 * i : 16 * side + 2 * i + 2, columns] = basis[:2, edge]

    own_z, (left, gain_l), (right, gain_r) = operators(BZ)
    zs_low = np.concatenate([np.tile(b[p : p + 2].T, (1, 16)) for b in (right, left) for p in (0, 2)], 1)
    zs_high = np.concatenate([np.tile(b[:2].T, (1, 32)) for b in (right, left)], 1)
    coarse_z = np.zeros((2, 384, 128), ml_dtypes.bfloat16)
    for p in range(2):
        coarse_z[p, :, 64 * p : 64 * p + 64] = three(own_z[128:].T, 0)
    coarse_z = coarse_z.reshape(768, 128)

    def spread(rows):
        k = rows.shape[1]
        fine = np.zeros((k, 256))
        fine[:, :64] = rows[:64].T
        fine[:, 128:192] = rows[64:128].T
        coarse = np.zeros((k, 128))
        coarse[:, :64] = rows[128:].T
        return fine, coarse

    main_fine, main_coarse = spread(own_z)
    halo_fine, halo_coarse = spread(np.concatenate([gain_l, gain_r], 1))

    def passes(main, halo):
        hi, lo = halves(main)
        ehi, elo = halves(halo)
        table = np.zeros((4, 512, main.shape[1]), ml_dtypes.bfloat16)
        for i in range(4):
            table[i, :384] = np.concatenate([hi, hi, lo], 0)
            table[i, 384 + 32 * i : 384 + 32 * i + 24] = np.concatenate([ehi, ehi, elo], 0)
        return table

    def places(first):
        p = np.zeros((4, 128, 128))
        for lane in range(128):
            i, s = lane // 2 % 4, first + lane % 2
            p[0, lane, 32 * i + s] = p[0, lane, 32 * i + 16 + s] = 1
            p[1, lane, 32 * i + 8 + s] = 1
            p[2, lane, 32 * i + 4 + s] = p[2, lane, 32 * i + 20 + s] = 1
            p[3, lane, 32 * i + 12 + s] = 1
        return p.reshape(512, 128).astype(ml_dtypes.bfloat16)

    wf, wc = passes(main_fine, halo_fine), passes(main_coarse, halo_coarse)
    send = (
        three(state_low, 1), three(state_high, 1), three(zs_low, 0), three(zs_high, 0), coarse_z, three(coarse_y, 1),
        three(y_low, 2), three(y_high, 2), three(y_more, 2).reshape(128, 48),
    )
    work = (
        three(z_one, 1), three(z_two, 1), three(y_high[2], 1), wf, wc,
        np.concatenate([places(0), places(2)], 0),
    )
    return send, work


def split(v):
    hi = v.astype(BF16)
    return hi, (v - hi.astype(F32)).astype(BF16)


def dot(a, b):
    return jnp.dot(a, b, preferred_element_type=F32)


def lift_loop(count, unroll, load, store):
    k = 2 * count
    s_a, d_a, s_b, d_b, s_c, d_c, s_d = [load(i % k) for i in range(k - 4, k + 3)]
    d_a = d_a + predict_one * (s_a + s_b)
    d_b = d_b + predict_one * (s_b + s_c)
    s_b = s_b + update_one * (d_a + d_b)
    d_c = d_c + predict_one * (s_c + s_d)
    s_c = s_c + update_one * (d_b + d_c)
    d_b = d_b + predict_two * (s_b + s_c)

    def step(j, carry):
        s_now, d_before, s_before, d_done = carry
        for u in range(unroll):
            n = unroll * j + u + 1
            d_now, s_next = load(lax.rem(2 * n + 1, k)), load(lax.rem(2 * n + 2, k))
            d_now = d_now + predict_one * (s_now + s_next)
            s_now = s_now + update_one * (d_before + d_now)
            d_before = d_before + predict_two * (s_before + s_now)
            s_before = s_before + update_two * (d_done + d_before)
            store(n - 1, s_before * scale_factor, d_before * (1.0 / scale_factor))
            s_now, d_before, s_before, d_done = s_next, d_now, s_now, d_before
        return s_now, d_before, s_before, d_done

    lax.fori_loop(0, count // unroll, step, (s_d, d_c, s_c, d_b))


def lift_x(v, x_hi, x_lo, rows):
    def store(n, low, high):
        x_hi[n, rows], x_lo[n, rows] = split(low)
        x_hi[HX + n, rows], x_lo[HX + n, rows] = split(high)

    lift_loop(HX, 16, lambda i: v[i, rows], store)


def find_y_states(x_hi, x_lo, st_low, st_high, coarse_z, y_send):
    more = [[], []]
    for half, table in ((0, st_low), (1, st_high)):
        n = 16
        for g in range(0, 8, 2):
            columns = []
            for u in (g, g + 1):
                parts = []
                for ref in (x_hi, x_lo):
                    for x in range(HX * half + 8 * u, HX * half + 8 * u + 8):
                        parts += [ref[x, 0:16], ref[x, 48:64]]
                columns.append(jnp.concatenate(parts + parts[:16], 0))
            states = dot(table[...], jnp.concatenate(columns, 1))
            for u in (0, 1):
                at = NX * half + n * (g + u)
                for side in (0, 1):
                    first = (n if half else 2 * n) * side
                    lanes = slice(128 * u, 128 * u + 128)
                    y_send[side, at : at + n] = states[first : first + n, lanes]
                    if not half:
                        more[side].append(states[first + n : first + 2 * n, lanes])
    pieces = []
    for part in range(2):
        hi, lo = split(jnp.concatenate(more[0][4 * part : 4 * part + 4] + more[1][4 * part : 4 * part + 4], 0))
        pieces += [hi, lo, hi]
    lifted = dot(jnp.concatenate(pieces, 1), coarse_z[...])
    y_send[0, 2 * NX :] = lifted[:HX]
    y_send[1, 2 * NX :] = lifted[HX:]


def find_z_states(x_hi, x_lo, zs_low, zs_high, coarse_y, z_send, z_raw):
    lane = lax.broadcasted_iota(jnp.int32, (8, 128), 1)

    def states_of(first, n, table, slot):
        hi = x_hi[first : first + n].reshape(n * BY, BZ)
        lo = x_lo[first : first + n].reshape(n * BY, BZ)
        states = dot(jnp.concatenate([hi, lo, hi], 1), table[...]).reshape(n, 8, 8, 128)
        acc = states[0]
        for i in range(1, n):
            acc = jnp.where((slot == i)[None], states[i], acc)
        return acc

    def gathered(pieces, of):
        width = 128 // len(pieces)
        out = None
        for k, piece in enumerate(pieces):
            turn = (width * (k - of)) % 128
            moved = pltpu.roll(piece, turn, 2) if turn else piece
            out = moved if out is None else jnp.where((lane // width == k)[None], moved, out)
        return out.reshape(64, 128)

    low = [states_of(16 * k, 16, zs_low, lane % 32 // 2) for k in range(4)]
    high = [states_of(HX + 32 * k, 32, zs_high, lane % 64 // 2) for k in range(2)]
    columns = []
    for side in range(2):
        z_send[side, 0:64] = gathered(low, 2 * side)
        z_send[side, 64:128] = gathered(high, side)
        second = gathered(low, 2 * side + 1)
        z_raw[side] = second
        hi, lo = split(second)
        columns.append(jnp.concatenate([hi, lo, hi], 0))
    lifted = dot(coarse_y[...], jnp.concatenate(columns, 1))
    z_send[0, 128:160] = lifted[:, :128]
    z_send[1, 128:160] = lifted[:, 128:]


def find_corners(z_send, z_raw, st_low, c_send):
    his, los = [], []
    zeros = jnp.zeros((32, 128), F32)
    for side in range(2):
        for top, low in (
            (z_send[side, 0:16], z_send[side, 48:64]),
            (z_raw[side, 0:16], z_raw[side, 48:64]),
            (z_send[side, 64:80], z_send[side, 112:128]),
            (zeros[:16], zeros[:16]),
        ):
            hi, lo = split(jnp.concatenate([top, low], 0))
            his.append(hi)
            los.append(lo)
    states = dot(st_low[...], jnp.concatenate(his + los + his, 0))
    for y in range(2):
        for z in range(2):
            for p in range(2):
                at = 32 * y + 16 * p + 8 * z
                c_send[2 * y + z, 8 * p : 8 * p + 8] = states[at : at + 8]


STEPS = [(-1, 0), (1, 0), (0, -1), (0, 1), (-1, -1), (-1, 1), (1, -1), (1, 1)]
ORDER = (0, 3, 1, 2)


def exchange_kernel(
    v_hbm, st_low_hbm, st_high_hbm, zs_low_hbm, zs_high_hbm, coarse_z_hbm, coarse_y_hbm,
    y_low_hbm, y_high_hbm, y_more_hbm,
    lhs_low, lhs_high, more, z_recv, c_recv,
    v, x_hi, x_lo, y_send, z_send, z_raw, c_send, y_recv,
    st_low, st_high, zs_low, zs_high, coarse_z, coarse_y, y_low, y_high, y_more, in_sem, send_sem, recv_sem,
):
    my_y, my_z = lax.axis_index("gy"), lax.axis_index("gz")
    n_y, n_z = lax.axis_size("gy"), lax.axis_size("gz")

    def device(step_y, step_z):
        return {
            "gy": lax.rem(my_y + step_y + n_y, n_y),
            "gz": lax.rem(my_z + step_z + n_z, n_z),
        }

    barrier = pltpu.get_barrier_semaphore()
    for step in STEPS:
        pl.semaphore_signal(barrier, inc=1, device_id=device(*step), device_id_type=MESH)

    def load(k, src, dst):
        copy = pltpu.make_async_copy(src, dst, in_sem.at[k])
        copy.start()
        return copy

    def load_rows(c):
        rows = pl.ds(16 * c, 16)
        return load(c, v_hbm.at[:, rows], v.at[:, rows])

    loads = {c: load_rows(c) for c in ORDER[:2]}
    tables = [
        (st_low_hbm, st_low), (st_high_hbm, st_high), (coarse_z_hbm, coarse_z), (zs_low_hbm, zs_low),
        (zs_high_hbm, zs_high), (coarse_y_hbm, coarse_y), (y_low_hbm, y_low), (y_high_hbm, y_high), (y_more_hbm, y_more),
    ]
    for k in (0, 1, 2):
        loads[4 + k] = load(4 + k, *tables[k])
    loads.update({c: load_rows(c) for c in ORDER[2:]})
    for k in range(3, 9):
        loads[4 + k] = load(4 + k, *tables[k])

    def lift(c):
        loads[c].wait()
        lift_x(v, x_hi, x_lo, pl.ds(16 * c, 16))

    def send(k):
        source = (y_send, z_send, c_send)[k // 2 if k < 4 else 2]
        target = (y_recv, z_recv, c_recv)[k // 2 if k < 4 else 2]
        at, to = (k % 2, 1 - k % 2) if k < 4 else (k - 4, 7 - k)
        copy = pltpu.make_async_remote_copy(
            src_ref=source.at[at], dst_ref=target.at[to],
            send_sem=send_sem.at[k], recv_sem=recv_sem.at[k],
            device_id=device(*STEPS[k]), device_id_type=MESH,
        )
        copy.start()
        return copy

    lift(ORDER[0])
    lift(ORDER[1])
    for k in (4, 5, 6):
        loads[k].wait()
    find_y_states(x_hi, x_lo, st_low, st_high, coarse_z, y_send)
    pl.semaphore_wait(barrier, 8)
    y_copies = [send(k) for k in (0, 1)]

    lift(ORDER[2])
    lift(ORDER[3])
    for k in (7, 8, 9):
        loads[k].wait()
    find_z_states(x_hi, x_lo, zs_low, zs_high, coarse_y, z_send, z_raw)
    find_corners(z_send, z_raw, st_low, c_send)
    z_copies = [send(k) for k in range(4, 8)]
    z_copies += [send(k) for k in (2, 3)]

    for k in (10, 11, 12):
        loads[k].wait()
    for copy in y_copies:
        copy.wait()
    lift_more(y_recv, y_more, more)
    for part in range(4):
        lift_y(part, True, x_hi, x_lo, y_recv, y_low, lhs_low)
        lift_y(part, False, x_hi, x_lo, y_recv, y_high, lhs_high)
    for copy in z_copies:
        copy.wait()


def stacked(hi, lo, tiles):
    thi, tlo = split(tiles)
    return jnp.concatenate([hi, thi, lo, tlo, hi, thi], 0)


def lift_z_halos(z_recv, c_recv, z_one, z_two, z_high, places, zh_low, zh_high):
    lane = lax.broadcasted_iota(jnp.int32, (1, 512), 1) % 128
    masks = [jnp.where(lane // 8 == g, 1.0, 0.0).astype(BF16) for g in range(16)]
    first, second, high = [], [], []
    for side in range(2):
        corners = [c_recv[2 * y + side, 8 * p : 8 * p + 8] for p in range(2) for y in range(2)]
        tiles = jnp.concatenate(corners, 0)
        own = z_recv[side]
        first += split(dot(z_one[...], tripled(jnp.concatenate([own[:64], tiles], 0))))
        second += split(own[128:160] + dot(z_two[...], tripled(tiles)))
        high += split(dot(z_high[...], tripled(jnp.concatenate([own[64:128], tiles[:16]], 0))))
    first, second, high = (jnp.concatenate(blocks, 1) for blocks in (first, second, high))
    one = jnp.concatenate([high * m for m in masks], 0)
    zh_high[...] = dot(one, places[:512]).astype(BF16).reshape(16, 64, 128)
    one = jnp.concatenate([first[:64] * m for m in masks], 0)
    zh_low[:, :64] = dot(one, places[:512]).astype(BF16).reshape(16, 64, 128)
    both = [jnp.concatenate([first[64:] * m, second * m], 1) for m in masks]
    both = dot(jnp.concatenate(both, 0), places[...])
    zh_low[:, 64:] = both.astype(BF16).reshape(16, 32, 128)


def tripled(v):
    hi, lo = split(v)
    return jnp.concatenate([hi, lo, hi], 0)


def lift_more(y_recv, y_more, more):
    for t in range(0, 8, 2):
        columns = []
        for u in (t, t + 1):
            at = 2 * NX + 8 * u
            columns.append(tripled(jnp.concatenate([y_recv[0, at : at + 8], y_recv[1, at : at + 8]], 0)))
        lifted = dot(y_more[...], jnp.concatenate(columns, 1))
        for u in (0, 1):
            for i in range(4):
                value = lifted[32 * i : 32 * i + 32, 128 * u : 128 * u + 128]
                x = 4 * (t + u) + i
                more[x] = value
                more[HX // 2 + x] = pltpu.roll(value, 64, 1)


def lift_y(part, low, x_hi, x_lo, y_recv, table, lhs):
    first = 0 if low else HX
    for i in range(4):
        for q in range(0, 4, 2):
            columns = []
            for u in (q, q + 1):
                x = first + 16 * part + 4 * u + i
                at = 8 * (x // 4)
                tiles = jnp.concatenate([y_recv[0, at : at + 8], y_recv[1, at : at + 8]], 0)
                columns.append(stacked(x_hi[x], x_lo[x], tiles))
            hi, lo = split(dot(table[i], jnp.concatenate(columns, 1)))
            for u in (0, 1):
                lhs[0, part, i, q + u] = hi[:, 128 * u : 128 * u + 128]
                lhs[1, part, i, q + u] = lo[:, 128 * u : 128 * u + 128]


def lift_z(part, i, zh, lhs, table, start, rows):
    hi = lhs[0, part, i, :, start : start + rows].reshape(4 * rows, 128)
    lo = lhs[1, part, i, :, start : start + rows].reshape(4 * rows, 128)
    zh = zh[4 * part : 4 * part + 4, start : start + rows].reshape(4 * rows, 128)
    return dot(jnp.concatenate([hi, lo, hi, zh], 1), table[i])


def low_part(part, lhs, more, zh_low, wf, wc, fine, level):
    for i in range(4):
        one = lift_z(part, i, zh_low, lhs, wf, 0, 64)
        two = lift_z(part, i, zh_low, lhs, wc, 64, 32)
        for q in range(4):
            x = 16 * part + 4 * q + i
            fine[0, x] = one[64 * q : 64 * q + 32, 128:192]
            fine[1, x] = one[64 * q + 32 : 64 * q + 64, :64]
            fine[2, x] = one[64 * q + 32 : 64 * q + 64, 128:192]
            level[x] = two[32 * q : 32 * q + 32] + more[x]


def high_part(part, lhs, zh_high, wf, fine):
    for i in range(4):
        one = lift_z(part, i, zh_high, lhs, wf, 0, 64)
        for q in range(4):
            x = 16 * part + 4 * q + i
            fine[3, x] = one[64 * q : 64 * q + 32, :64]
            fine[4, x] = one[64 * q : 64 * q + 32, 128:192]
            fine[5, x] = one[64 * q + 32 : 64 * q + 64, :64]
            fine[6, x] = one[64 * q + 32 : 64 * q + 64, 128:192]


def lift_level(level, coarse):
    def store(n, low, high):
        for bx, value in enumerate((low, high)):
            for by in range(2):
                for bz in range(2):
                    coarse[4 * bx + 2 * by + bz, n] = value[
                        16 * by : 16 * by + 16, 32 * bz : 32 * bz + 32
                    ]

    lift_loop(HX // 2, 32, lambda i: level[i], store)


def finish_kernel(
    lhs_low, lhs_high, more, z_recv, c_recv, z_one, z_two, z_high, wf, wc, places,
    fine_hbm, coarse_hbm,
    fine, coarse, level, zh_low, zh_high, sem,
):
    copies = []

    def write(bands, part):
        at = pl.ds(16 * part, 16)
        src, dst = fine.at[pl.ds(*bands), at], fine_hbm.at[pl.ds(*bands), at]
        copies.append(pltpu.make_async_copy(src, dst, sem.at[part + (4 if bands == HIGH_BANDS else 0)]))
        copies[-1].start()

    lift_z_halos(z_recv, c_recv, z_one, z_two, z_high, places, zh_low, zh_high)

    def low(part):
        low_part(part, lhs_low, more, zh_low, wf, wc, fine, level)
        write(LOW_BANDS, part)

    def high(part):
        high_part(part, lhs_high, zh_high, wf, fine)
        write(HIGH_BANDS, part)

    def last():
        lift_level(level, coarse)
        copies.append(pltpu.make_async_copy(coarse, coarse_hbm, sem.at[8]))
        copies[-1].start()

    high(0)
    high(1)
    low(0)
    low(1)
    low(2)
    low(3)
    last()
    high(2)
    high(3)
    for copy in copies:
        copy.wait()


LOW_BANDS, HIGH_BANDS = (0, 3), (3, 4)


def body(velocity):
    send, work = constants()
    vmem = pl.BlockSpec(memory_space=pltpu.VMEM)
    hbm = pl.BlockSpec(memory_space=pltpu.HBM)
    shape = jax.ShapeDtypeStruct
    y_shape, z_shape, c_shape = (2, Y_ROWS, BZ), (2, Z_ROWS, 128), (4, 16, 128)
    halos = pl.pallas_call(
        exchange_kernel,
        out_shape=(
            shape((2, 4, 4, 4, 96, 128), BF16), shape((2, 4, 4, 4, 64, 128), BF16),
            shape((HX, 32, 128), F32), shape(z_shape, F32), shape(c_shape, F32),
        ),
        in_specs=[hbm] * 10,
        out_specs=(vmem,) * 5,
        scratch_shapes=[
            pltpu.VMEM((NX, BY, BZ), F32),
            pltpu.VMEM((NX, BY, BZ), BF16),
            pltpu.VMEM((NX, BY, BZ), BF16),
            pltpu.VMEM(y_shape, F32),
            pltpu.VMEM(z_shape, F32),
            pltpu.VMEM((2, BY, 128), F32),
            pltpu.VMEM(c_shape, F32),
            pltpu.VMEM(y_shape, F32),
            *[pltpu.VMEM(a.shape, BF16) for a in send],
            pltpu.SemaphoreType.DMA((13,)),
            pltpu.SemaphoreType.DMA((8,)),
            pltpu.SemaphoreType.DMA((8,)),
        ],
        compiler_params=pltpu.CompilerParams(
            collective_id=0, has_side_effects=True, vmem_limit_bytes=32 * 2**20
        ),
        name="exchange",
    )(*[pltpu.with_memory_space_constraint(jnp.asarray(a), pltpu.HBM) for a in (velocity, *send)])
    fine_shape, coarse_shape = (7, HX, BY // 2, BZ // 2), (8, HX // 2, BY // 4, BZ // 4)
    return pl.pallas_call(
        finish_kernel,
        out_shape=(shape(fine_shape, F32), shape(coarse_shape, F32)),
        in_specs=[vmem] * 11,
        out_specs=(hbm, hbm),
        scratch_shapes=[
            pltpu.VMEM(fine_shape, F32),
            pltpu.VMEM(coarse_shape, F32),
            pltpu.VMEM((HX, 32, 128), F32),
            pltpu.VMEM((16, 96, 128), BF16),
            pltpu.VMEM((16, 64, 128), BF16),
            pltpu.SemaphoreType.DMA((9,)),
        ],
        compiler_params=pltpu.CompilerParams(vmem_limit_bytes=28 * 2**20),
        name="finish",
    )(*halos, *[jnp.asarray(a) for a in work])


def solution(mesh):
    return jax.shard_map(
        body,
        mesh=mesh,
        in_specs=(P(None, "gy", "gz"),),
        out_specs=(P(None, None, "gy", "gz"), P(None, None, "gy", "gz")),
        check_vma=False,
    )
```
